512 devices in a mesh: tm: 4 (over x), space: 128 (over z, y, core).
Axes of the slice: x: 4, y: 8, z: 8, core: 2. Of those that a mesh axis runs over, the one named last changes fastest.
Arguments:
- bases: bfloat16 [4, 32768, 256], P('tm', 'space'), may hold values from -8 to 8
Outputs:
- merged_basis: float32 [32768, 256], P('space', 'tm')
The draws below stay inside these ranges and needn't reach their ends.
All inputs are finite; a program needn't handle non-finite values.
Results may differ from the reference program's by a relative error of at most 0.0081.
Values may be sent and summed in bfloat16 or wider, within the bound.
A program may use at most 64 MiB of HBM per device.

```python
import math
import jax
import jax.numpy as jnp
from jax import lax

K = 256
ITERS = 2
GRID = 32768
PERIODS = 4


def draw_bases(key, part):
    key = jax.random.fold_in(key, 1)
    key_rate, key_rough, key_rows, key_own, key_shared, key_mix, key_shmix = jax.random.split(key, 7)
    rates = jax.random.uniform(key_rate, (PERIODS, 1, 1), jnp.float32, 0.5, 1.5)
    modes = jnp.arange(K, dtype=jnp.float32).reshape(1, 1, K) / K
    rough = jax.random.uniform(key_rough, (PERIODS, 1, K), jnp.float32, 0.7, 1.3)
    spectrum = jnp.exp(-1.4 * rates * modes) * rough
    row_scale = jax.random.uniform(key_rows, (1, GRID, 1), jnp.float32, 0.5, 1.5)
    own_field = jax.random.randint(key_own, (PERIODS, GRID, K), -4, 5).astype(jnp.float32)
    shared_field = jax.random.randint(key_shared, (GRID, K), -4, 5).astype(jnp.float32)
    own_mixing = jax.random.randint(key_mix, (PERIODS, K, K), -1, 2).astype(jnp.float32)
    shared_mixing = jax.random.randint(key_shmix, (K, K), -1, 2).astype(jnp.float32)
    own_part = jnp.einsum('pgk,pkj->pgj', own_field, own_mixing, precision=lax.Precision.HIGHEST)
    shared_part = jnp.dot(shared_field, shared_mixing, precision=lax.Precision.HIGHEST).reshape(1, GRID, K)
    unit = 1.0 / math.sqrt(20.0 / 3.0 * (2.0 * K / 3.0))
    mixed = unit * own_part + 0.7 * unit * shared_part
    return jnp.clip(mixed * spectrum * row_scale, -8.0, 8.0).astype(jnp.bfloat16)


def setup_inputs(seed: int = 0) -> dict:
    key_of = jax.random.split(jax.random.key(seed), 2)
    return {
        "bases": draw_bases(jax.random.fold_in(key_of[1], 71), 0),
    }


def rotate(gram_matrix):
    half_width = gram_matrix.shape[0] // 2
    identity = jnp.eye(half_width, dtype=jnp.float32)
    frame = jnp.concatenate([identity, identity], 0)
    for iteration in range(ITERS):
        image_block = jnp.dot(gram_matrix, frame, precision=lax.Precision.HIGHEST)
        metric = jnp.dot(image_block.T, jnp.dot(gram_matrix, image_block, precision=lax.Precision.HIGHEST), precision=lax.Precision.HIGHEST)
        factor = jnp.linalg.cholesky(metric)
        frame = lax.linalg.triangular_solve(factor, image_block, left_side=False, lower=True, transpose_a=True)
    applied = jnp.dot(gram_matrix, frame, precision=lax.Precision.HIGHEST)
    energy = jnp.dot(applied.T, applied, precision=lax.Precision.HIGHEST)
    scale_factor = jnp.linalg.cholesky(energy)
    return jnp.dot(frame, scale_factor, precision=lax.Precision.HIGHEST)

def merge(lower_basis, upper_basis):
    stacked = jnp.concatenate([lower_basis, upper_basis], 1)
    gram_matrix = jnp.dot(stacked.T.astype(jnp.float32), stacked.astype(jnp.float32), preferred_element_type=jnp.float32) / GRID
    rotation = rotate(gram_matrix).astype(jnp.bfloat16)
    return jnp.dot(stacked.astype(jnp.float32), rotation.astype(jnp.float32), preferred_element_type=jnp.float32)

def reference(bases):
    first = merge(bases[0], bases[1]).astype(jnp.bfloat16)
    second = merge(bases[2], bases[3]).astype(jnp.bfloat16)
    return merge(first, second)
```

```python
import functools

import jax
import jax.numpy as jnp
from jax import lax
from jax.experimental import pallas as pl
from jax.experimental.pallas import tpu as pltpu
from jax.sharding import PartitionSpec as P

MESH = pl.DeviceIdType.MESH
F32 = jnp.float32
BF16 = jnp.bfloat16
K = 256
H = 128
GRID = 32768
CHUNK = 40
ROWS = 1280
QUARTER = ROWS // 4
HALF = ROWS // 2
VMEM_LIMIT = 48 * 1024 * 1024


def dot(a, b, dims=((1,), (0,))):
    return lax.dot_general(
        a,
        b,
        (dims, ((), ())),
        precision=lax.Precision.HIGHEST,
        preferred_element_type=F32,
    )


def dot_nt(a, b):
    return dot(a, b, ((1,), (1,)))


def dot_tn(a, b):
    return dot(a, b, ((0,), (0,)))


def lane_bc(x, c):
    return jnp.broadcast_to(x[:, c : c + 1], x.shape)


def sub_bc(x, r):
    return jnp.broadcast_to(x[r : r + 1, :], x.shape)


def weighted(cols, rows):
    s0 = cols[0] * rows[0]
    s1 = cols[1] * rows[1]
    for c in range(2, 8, 2):
        s0 = s0 + cols[c] * rows[c]
        s1 = s1 + cols[c + 1] * rows[c + 1]
    return s0 + s1


def factor_steps(a, pending_per_step=2):
    n = a.shape[0]
    groups = n // 8
    sub = lax.broadcasted_iota(jnp.int32, (8, n), 0)
    lane = lax.broadcasted_iota(jnp.int32, (8, n), 1)
    g_rows = [a[8 * g : 8 * g + 8] for g in range(groups)]
    x_rows = [jnp.where(lane == sub + 8 * g, 1.0, 0.0).astype(F32) for g in range(groups)]
    upper, inverse, pending = [], [], []

    def update(h, g, v_a, v_x):
        cols = [lane_bc(g_rows[h], 8 * g + c) for c in range(8)]
        g_rows[h] = g_rows[h] - weighted(cols, v_a)
        x_rows[h] = x_rows[h] - weighted(cols, v_x)

    for g in range(groups):
        p = [lane_bc(g_rows[g], 8 * g + c) for c in range(8)]
        jordan = forward = g_rows[g]
        jordan_x = forward_x = x_rows[g]
        recips = jnp.ones_like(jordan)
        for j in range(8):
            r = 1.0 / sub_bc(p[j], j)
            f = p[j] * r
            f_all = jnp.where(sub != j, f, 0.0)
            f_below = jnp.where(sub > j, f, 0.0)
            for c in range(j + 1, 8):
                p[c] = p[c] - f_all * sub_bc(p[c], j)
            w, w_x = sub_bc(jordan, j), sub_bc(jordan_x, j)
            jordan = jordan - f_all * w
            jordan_x = jordan_x - f_all * w_x
            if j < 7:
                forward = forward - f_below * w
                forward_x = forward_x - f_below * w_x
            recips = jnp.where(sub == j, r, recips)
            for _ in range(pending_per_step):
                if pending:
                    update(*pending.pop(0))
            yield None
        while pending:
            update(*pending.pop(0))
        root = jnp.sqrt(recips)
        upper.append(jnp.where(lane >= sub + 8 * g, forward * root, 0.0))
        inverse.append(forward_x * root)
        if g < groups - 1:
            v, v_xx = jordan * recips, jordan_x * recips
            v_a = [sub_bc(v, c) for c in range(8)]
            v_x = [sub_bc(v_xx, c) for c in range(8)]
            update(g + 1, g, v_a, v_x)
            pending = [(h, g, v_a, v_x) for h in range(g + 2, groups)]
    yield jnp.concatenate(upper, 0), jnp.concatenate(inverse, 0)


def run_together(*steps):
    result = None
    for result in zip(*steps):
        pass
    return result


def cholesky_pieces(matrices):
    first = run_together(*[factor_steps(m[:H, :H]) for m in matrices])
    u12 = [dot(l1, m[:H, H:]) for (_, l1), m in zip(first, matrices)]
    rest = [m[H:, H:] - dot_tn(u, u) for m, u in zip(matrices, u12)]
    second = run_together(*[factor_steps(s) for s in rest])
    pieces = []
    for (u11, l1), u, (u22, l2) in zip(first, u12, second):
        x21 = -dot(l2, dot_tn(u, l1))
        zero = jnp.zeros((H, H), F32)
        inverse = jnp.concatenate(
            [jnp.concatenate([l1, zero], 1), jnp.concatenate([x21, l2], 1)], 0
        )
        upper = jnp.concatenate(
            [jnp.concatenate([u11, u], 1), jnp.concatenate([zero, u22], 1)], 0
        )
        pieces.append((upper, inverse))
    return pieces


def unpack_gram(packed_ref, gram_ref):
    scale = 1.0 / GRID
    b = [packed_ref[H * i : H * i + H, :] * scale for i in range(10)]
    at = {
        (0, 0): b[0], (1, 0): b[1], (0, 1): b[1].T, (1, 1): b[2],
        (2, 2): b[3], (3, 2): b[4], (2, 3): b[4].T, (3, 3): b[5],
        (0, 2): b[6], (0, 3): b[7], (1, 2): b[8], (1, 3): b[9],
        (2, 0): b[6].T, (3, 0): b[7].T, (2, 1): b[8].T, (3, 1): b[9].T,
    }
    for (r, c), block in at.items():
        gram_ref[H * r : H * r + H, H * c : H * c + H] = block


def rotation_transposed(gram_ref):
    gram = gram_ref[...]
    y1 = gram[:K] + gram[K:]
    z1 = dot(y1, gram)
    ((_, inv1),) = cholesky_pieces([dot_nt(y1, z1)])
    y2 = dot(inv1, z1)
    a2 = dot(y2, gram)
    (_, inv2), (upper, _) = cholesky_pieces([dot_nt(y2, a2), dot_nt(a2, a2)])
    f2 = dot(inv2, y2)
    s = dot_nt(upper, inv2)
    return dot(s, f2).astype(BF16)


def merge_kernel(last, packed_ref, stacked_ref, out_ref, gram_ref, rot_ref):
    unpack_gram(packed_ref, gram_ref)
    rot_ref[...] = rotation_transposed(gram_ref)
    if last:
        width = out_ref.shape[1]
        start = pl.multiple_of(lax.axis_index("tm") * width, width)
        rot = rot_ref[pl.ds(start, width), :]
    else:
        rot = rot_ref[...]
    nt = (((1,), (1,)), ((), ()))
    merged = lax.dot_general(
        stacked_ref[0], rot[:, :K], nt, preferred_element_type=F32
    ) + lax.dot_general(stacked_ref[1], rot[:, K:], nt, preferred_element_type=F32)
    out_ref[...] = merged.astype(out_ref.dtype)


def merge(packed, stacked, last):
    out = jax.ShapeDtypeStruct((256, 64), F32) if last else jax.ShapeDtypeStruct((256, K), BF16)
    return pl.pallas_call(
        functools.partial(merge_kernel, last),
        out_shape=out,
        in_specs=[pl.BlockSpec(memory_space=pltpu.VMEM)] * 2,
        out_specs=pl.BlockSpec(memory_space=pltpu.VMEM),
        scratch_shapes=[pltpu.VMEM((2 * K, 2 * K), F32), pltpu.VMEM((K, 2 * K), BF16)],
        compiler_params=pltpu.CompilerParams(vmem_limit_bytes=VMEM_LIMIT),
        name="merge_last" if last else "merge_pair",
    )(packed, stacked)


def gram_kernel(
    level, own_ref, packed_ref, stacked_ref, part, half, recv0, recv1, sum1, recv2,
    x_sem, core_sem, sem1, sem2, sem3, sem4,
):
    tm, space = lax.axis_index("tm"), lax.axis_index("space")
    core, y, z = lax.rem(space, 2), lax.rem(lax.div(space, 2), 8), lax.div(space, 16)
    partner_tm = tm + 1 - 2 * lax.rem(tm, 2) if level == 0 else 3 - tm
    slot = lax.rem(tm, 2) if level == 0 else lax.div(tm, 2)
    sibling = (tm, space + 1 - 2 * core)
    partner = (partner_tm, space)

    def on_y(d):
        p = lax.rem(y + d, 8)
        return p, (tm, (z * 8 + p) * 2 + core)

    def on_z(d):
        p = lax.rem(z + d, 8)
        return p, (tm, (p * 8 + y) * 2 + core)

    first_axis, second_axis = (on_y, on_z), (on_z, on_y)
    first_at, second_at = (y, z), (z, y)

    barrier = pltpu.get_barrier_semaphore()
    others = [sibling, partner]
    for d in range(1, 8):
        others += [on_y(d)[1], on_z(d)[1]]
    for device in others:
        pl.semaphore_signal(barrier, inc=1, device_id=device, device_id_type=MESH)
    pl.semaphore_wait(barrier, len(others))

    def remote(src, dst, sems, index, device):
        copy = pltpu.make_async_remote_copy(
            src_ref=src, dst_ref=dst, send_sem=sems.at[(0,) + index],
            recv_sem=sems.at[(1,) + index], device_id=device, device_id_type=MESH,
        )
        copy.start()
        return copy

    def rows(start, count):
        return pl.ds(pl.multiple_of(start, 8), count)

    exchange = remote(own_ref, stacked_ref.at[slot], x_sem, (0,), partner)
    stacked_ref[slot] = own_ref[...]
    exchange.wait()

    tn = (((0,), (0,)), ((), ()))
    low, high = stacked_ref[0], stacked_ref[1]
    for base, block in ((0, (low, low)), (3, (high, high)), (6, (low, high))):
        g = lax.dot_general(block[0], block[1], tn, preferred_element_type=F32)
        places = ((0, 0), (1, 0), (1, 1)) if base < 6 else ((0, 0), (0, 1), (1, 0), (1, 1))
        for i, (r, c) in enumerate(places):
            at = H * (base + i)
            part[at : at + H, :] = g[H * r : H * r + H, H * c : H * c + H]

    to_sibling = remote(part.at[rows((1 - core) * HALF, HALF)], recv0, core_sem, (0,), sibling)
    to_sibling.wait()
    half[...] = part[rows(core * HALF, HALF), :] + recv0[...]

    copies = []
    for d in range(1, 8):
        for h in range(2):
            p, device = first_axis[h](d)
            copies.append(
                remote(
                    half.at[rows(h * QUARTER + p * CHUNK, CHUNK)],
                    recv1.at[h, first_at[h]], sem1, (h, d), device,
                )
            )
    for h in range(2):
        recv1[h, first_at[h]] = half[rows(h * QUARTER + first_at[h] * CHUNK, CHUNK), :]
    for copy in copies:
        copy.wait()
    for h in range(2):
        total = recv1[h, 0]
        for p in range(1, 8):
            total = total + recv1[h, p]
        sum1[h] = total

    copies = []
    for d in range(1, 8):
        for h in range(2):
            _, device = second_axis[h](d)
            copies.append(
                remote(sum1.at[h], recv2.at[h, second_at[h]], sem2, (h, d), device)
            )
    for h in range(2):
        recv2[h, second_at[h]] = sum1[h]
    for copy in copies:
        copy.wait()

    def place(h, p):
        return rows(core * HALF + h * QUARTER + p * CHUNK, CHUNK)

    for h in range(2):
        total = recv2[h, 0]
        for p in range(1, 8):
            total = total + recv2[h, p]
        packed_ref[place(h, first_at[h]), :] = total

    copies = []
    for d in range(1, 8):
        for h in range(2):
            _, device = first_axis[h](d)
            mine = packed_ref.at[place(h, first_at[h])]
            copies.append((h, d, remote(mine, mine, sem3, (h, d), device)))
    forwards = []
    for h in range(2):
        mine = packed_ref.at[place(h, first_at[h])]
        forwards.append(remote(mine, mine, sem4, (h, 0), sibling))
    for h, d, copy in copies:
        copy.wait()
        p = lax.rem(first_at[h] + 8 - d, 8)
        arrived = packed_ref.at[place(h, p)]
        forwards.append(remote(arrived, arrived, sem4, (h, d), sibling))
    for copy in forwards:
        copy.wait()


def gram(own, level):
    dma = pltpu.SemaphoreType.DMA
    return pl.pallas_call(
        functools.partial(gram_kernel, level),
        out_shape=(
            jax.ShapeDtypeStruct((ROWS, H), F32),
            jax.ShapeDtypeStruct((2, 256, K), BF16),
        ),
        in_specs=[pl.BlockSpec(memory_space=pltpu.VMEM)],
        out_specs=[pl.BlockSpec(memory_space=pltpu.VMEM)] * 2,
        scratch_shapes=[
            pltpu.VMEM((ROWS, H), F32),
            pltpu.VMEM((HALF, H), F32),
            pltpu.VMEM((HALF, H), F32),
            pltpu.VMEM((2, 8, CHUNK, H), F32),
            pltpu.VMEM((2, CHUNK, H), F32),
            pltpu.VMEM((2, 8, CHUNK, H), F32),
            dma((2, 1)),
            dma((2, 1)),
            dma((2, 2, 8)),
            dma((2, 2, 8)),
            dma((2, 2, 8)),
            dma((2, 2, 8)),
        ],
        compiler_params=pltpu.CompilerParams(
            collective_id=level, has_side_effects=True, vmem_limit_bytes=VMEM_LIMIT
        ),
        name="gram_pair" if level == 0 else "gram_last",
    )(own)


def body(bases):
    packed, stacked = gram(bases[0], 0)
    current = merge(packed, stacked, False)
    packed, stacked = gram(current, 1)
    return merge(packed, stacked, True)


def solution(mesh):
    return jax.shard_map(
        body,
        mesh=mesh,
        in_specs=(P("tm", "space", None),),
        out_specs=P("space", "tm"),
        check_vma=False,
    )
```

```python
import functools

import jax
import jax.numpy as jnp
from jax import lax
from jax.experimental import pallas as pl
from jax.experimental.pallas import tpu as pltpu
from jax.sharding import PartitionSpec as P

MESH = pl.DeviceIdType.MESH
F32 = jnp.float32
BF16 = jnp.bfloat16
K = 256
H = 128
GRID = 32768
PAIR_ROWS = 40
CROSS_ROWS = 16
CHUNK = PAIR_ROWS + CROSS_ROWS
CHUNKS = 32
PAIR = PAIR_ROWS * CHUNKS
CROSS = CROSS_ROWS * CHUNKS
ROWS = CHUNK * CHUNKS
QUARTER = ROWS // 4
HALF = ROWS // 2
FAR_FIRST = (4, 3, 5, 2, 6, 1, 7)
VMEM_LIMIT = 48 * 1024 * 1024


def dot(a, b, dims=((1,), (0,))):
    return lax.dot_general(
        a,
        b,
        (dims, ((), ())),
        precision=lax.Precision.HIGHEST,
        preferred_element_type=F32,
    )


def dot_nt(a, b):
    return dot(a, b, ((1,), (1,)))


def dot_tn(a, b):
    return dot(a, b, ((0,), (0,)))


def lane_bc(x, c):
    return jnp.broadcast_to(x[:, c : c + 1], x.shape)


def sub_bc(x, r):
    return jnp.broadcast_to(x[r : r + 1, :], x.shape)


def weighted(cols, rows):
    s0 = cols[0] * rows[0]
    s1 = cols[1] * rows[1]
    for c in range(2, 8, 2):
        s0 = s0 + cols[c] * rows[c]
        s1 = s1 + cols[c + 1] * rows[c + 1]
    return s0 + s1


def factor_steps(a, pending_per_step=2):
    n = a.shape[0]
    groups = n // 8
    sub = lax.broadcasted_iota(jnp.int32, (8, n), 0)
    lane = lax.broadcasted_iota(jnp.int32, (8, n), 1)
    g_rows = [a[8 * g : 8 * g + 8] for g in range(groups)]
    x_rows = [jnp.where(lane == sub + 8 * g, 1.0, 0.0).astype(F32) for g in range(groups)]
    upper, inverse, pending = [], [], []

    def update(h, g, v_a, v_x):
        cols = [lane_bc(g_rows[h], 8 * g + c) for c in range(8)]
        g_rows[h] = g_rows[h] - weighted(cols, v_a)
        x_rows[h] = x_rows[h] - weighted(cols, v_x)

    for g in range(groups):
        p = [lane_bc(g_rows[g], 8 * g + c) for c in range(8)]
        jordan = forward = g_rows[g]
        jordan_x = forward_x = x_rows[g]
        recips = jnp.ones_like(jordan)
        for j in range(8):
            r = 1.0 / sub_bc(p[j], j)
            f = p[j] * r
            f_all = jnp.where(sub != j, f, 0.0)
            f_below = jnp.where(sub > j, f, 0.0)
            for c in range(j + 1, 8):
                p[c] = p[c] - f_all * sub_bc(p[c], j)
            w, w_x = sub_bc(jordan, j), sub_bc(jordan_x, j)
            jordan = jordan - f_all * w
            jordan_x = jordan_x - f_all * w_x
            if j < 7:
                forward = forward - f_below * w
                forward_x = forward_x - f_below * w_x
            recips = jnp.where(sub == j, r, recips)
            for _ in range(pending_per_step):
                if pending:
                    update(*pending.pop(0))
            yield None
        while pending:
            update(*pending.pop(0))
        root = jnp.sqrt(recips)
        upper.append(jnp.where(lane >= sub + 8 * g, forward * root, 0.0))
        inverse.append(forward_x * root)
        if g < groups - 1:
            v, v_xx = jordan * recips, jordan_x * recips
            v_a = [sub_bc(v, c) for c in range(8)]
            v_x = [sub_bc(v_xx, c) for c in range(8)]
            update(g + 1, g, v_a, v_x)
            pending = [(h, g, v_a, v_x) for h in range(g + 2, groups)]
    yield jnp.concatenate(upper, 0), jnp.concatenate(inverse, 0)


def run_together(*steps):
    result = None
    for result in zip(*steps):
        pass
    return result


def cholesky_pieces(matrices):
    first = run_together(*[factor_steps(m[:H, :H]) for m in matrices])
    u12 = [dot(l1, m[:H, H:]) for (_, l1), m in zip(first, matrices)]
    rest = [m[H:, H:] - dot_tn(u, u) for m, u in zip(matrices, u12)]
    second = run_together(*[factor_steps(s) for s in rest])
    pieces = []
    for (u11, l1), u, (u22, l2) in zip(first, u12, second):
        x21 = -dot(l2, dot_tn(u, l1))
        zero = jnp.zeros((H, H), F32)
        inverse = jnp.concatenate(
            [jnp.concatenate([l1, zero], 1), jnp.concatenate([x21, l2], 1)], 0
        )
        upper = jnp.concatenate(
            [jnp.concatenate([u11, u], 1), jnp.concatenate([zero, u22], 1)], 0
        )
        pieces.append((upper, inverse))
    return pieces


def split3(x):
    hi = x.astype(BF16)
    rest = x - hi.astype(F32)
    mid = rest.astype(BF16)
    low = (rest - mid.astype(F32)).astype(BF16)
    return hi, mid, low


def bf_dot(a, b, dims=((1,), (0,))):
    return lax.dot_general(a, b, (dims, ((), ())), preferred_element_type=F32)


def rounded_left(a, x):
    hi, mid, low = split3(x)
    return bf_dot(a, low) + bf_dot(a, mid) + bf_dot(a, hi)


def rounded_right_nt(x, a):
    nt = ((1,), (1,))
    hi, mid, low = split3(x)
    return bf_dot(low, a, nt) + bf_dot(mid, a, nt) + bf_dot(hi, a, nt)


def put(ref, r, c, block):
    ref[H * r : H * r + H, H * c : H * c + H] = block


def unpack_pair(packed_ref, gram_ref):
    b = [packed_ref[H * i : H * i + H, :] * (1.0 / GRID) for i in range(10)]
    for base, at in ((0, 0), (3, 2)):
        put(gram_ref, at, at, b[base])
        put(gram_ref, at + 1, at, b[base + 1])
        put(gram_ref, at, at + 1, b[base + 1].T)
        put(gram_ref, at + 1, at + 1, b[base + 2])
    for i, (r, c) in enumerate(((0, 2), (0, 3), (1, 2), (1, 3))):
        put(gram_ref, r, c, b[6 + i])
        put(gram_ref, c, r, b[6 + i].T)


CROSS_AT = ((0, 1), (1, 0), (1, 1), (0, 0))


def unpack_cross(cross_ref, gram_ref):
    for plane, (r, c) in enumerate(CROSS_AT):
        for i, (rr, cc) in enumerate(((0, 0), (0, 1), (1, 0), (1, 1))):
            for k in range(H // CROSS_ROWS):
                chunk = i * (H // CROSS_ROWS) + k
                at = (chunk * 4 + plane) * CROSS_ROWS
                top, left = K * r + H * rr + CROSS_ROWS * k, K * c + H * cc
                gram_ref[top : top + CROSS_ROWS, left : left + H] = cross_ref[
                    at : at + CROSS_ROWS, :
                ] * (1.0 / GRID)


def rotation_transposed(gram_ref):
    gram = gram_ref[...]
    y1 = gram[:K] + gram[K:]
    z1 = dot(y1, gram)
    ((_, inv1),) = cholesky_pieces([dot_nt(y1, z1)])
    y2 = dot(inv1, z1)
    a2 = dot(y2, gram)
    (_, inv2), (upper, _) = cholesky_pieces([dot_nt(y2, a2), dot_nt(a2, a2)])
    f2 = dot(inv2, y2)
    s = dot_nt(upper, inv2)
    return dot(s, f2).astype(BF16)


def merge_pair_kernel(packed_ref, stacked_ref, rot_ref, out_ref, diag_ref, gram_ref):
    unpack_pair(packed_ref, gram_ref)
    rot = rotation_transposed(gram_ref)
    rot_ref[...] = rot
    nt = ((1,), (1,))
    out_ref[...] = (
        bf_dot(stacked_ref[0], rot[:, :K], nt) + bf_dot(stacked_ref[1], rot[:, K:], nt)
    ).astype(BF16)
    diag = rounded_right_nt(rounded_left(rot, gram_ref[...]), rot)
    for i, (r, c) in enumerate(((0, 0), (1, 0), (1, 1))):
        diag_ref[H * i : H * i + H, :] = diag[H * r : H * r + H, H * c : H * c + H]


def merge_pair(packed, stacked):
    vmem = pl.BlockSpec(memory_space=pltpu.VMEM)
    return pl.pallas_call(
        merge_pair_kernel,
        out_shape=(
            jax.ShapeDtypeStruct((K, 2 * K), BF16),
            jax.ShapeDtypeStruct((256, K), BF16),
            jax.ShapeDtypeStruct((3 * H, H), F32),
        ),
        in_specs=[vmem] * 2,
        out_specs=[vmem] * 3,
        scratch_shapes=[pltpu.VMEM((2 * K, 2 * K), F32)],
        compiler_params=pltpu.CompilerParams(vmem_limit_bytes=VMEM_LIMIT),
        name="merge_pair",
    )(packed, stacked)


def merge_last_kernel(cross_ref, rots_ref, rows_ref, diags_ref, out_ref, gram_ref, rot_ref):
    unpack_cross(cross_ref, gram_ref)
    cross = rounded_right_nt(rounded_left(rots_ref[0], gram_ref[...]), rots_ref[1])
    gram_ref[:K, K:] = cross
    gram_ref[K:, :K] = cross.T
    for i in range(2):
        b = [diags_ref[i, H * k : H * k + H, :] for k in range(3)]
        put(gram_ref, 2 * i, 2 * i, b[0])
        put(gram_ref, 2 * i + 1, 2 * i, b[1])
        put(gram_ref, 2 * i, 2 * i + 1, b[1].T)
        put(gram_ref, 2 * i + 1, 2 * i + 1, b[2])
    rot_ref[...] = rotation_transposed(gram_ref)
    width = out_ref.shape[1]
    start = pl.multiple_of(lax.axis_index("tm") * width, width)
    rot = rot_ref[pl.ds(start, width), :]
    nt = ((1,), (1,))
    out_ref[...] = bf_dot(rows_ref[0], rot[:, :K], nt) + bf_dot(rows_ref[1], rot[:, K:], nt)


def merge_last(cross, rots, rows, diags):
    vmem = pl.BlockSpec(memory_space=pltpu.VMEM)
    return pl.pallas_call(
        merge_last_kernel,
        out_shape=jax.ShapeDtypeStruct((256, 64), F32),
        in_specs=[vmem] * 4,
        out_specs=vmem,
        scratch_shapes=[pltpu.VMEM((2 * K, 2 * K), F32), pltpu.VMEM((K, 2 * K), BF16)],
        compiler_params=pltpu.CompilerParams(vmem_limit_bytes=VMEM_LIMIT),
        name="merge_last",
    )(cross, rots, rows, diags)


def enter(devices):
    barrier = pltpu.get_barrier_semaphore()
    for device in devices:
        pl.semaphore_signal(barrier, inc=1, device_id=device, device_id_type=MESH)
    pl.semaphore_wait(barrier, len(devices))


def remote(src, dst, sems, index, device):
    copy = pltpu.make_async_remote_copy(
        src_ref=src,
        dst_ref=dst,
        send_sem=sems.at[(0,) + index],
        recv_sem=sems.at[(1,) + index],
        device_id=device,
        device_id_type=MESH,
    )
    copy.start()
    return copy


def span(start, count):
    return pl.ds(pl.multiple_of(start, 8), count)


def store_pieces(part, block, first, per_chunk, offset):
    row = 0
    while row < block.shape[0]:
        chunk, at = divmod(first + row, per_chunk)
        count = min(per_chunk - at, block.shape[0] - row)
        to = chunk * CHUNK + offset + at
        part[to : to + count, :] = block[row : row + count]
        row += count


def gram_kernel(
    own_ref, packed_ref, cross_ref, stacked_ref, across, part, half, recv0, recv1, sum1, recv2,
    x_sem, core_sem, sem1, sem2, sem_pair, sem_pair_core, sem_x, sem_cross, sem_cross_core,
):
    tm, space = lax.axis_index("tm"), lax.axis_index("space")
    core, y, z = lax.rem(space, 2), lax.rem(lax.div(space, 2), 8), lax.div(space, 16)
    slot = lax.rem(tm, 2)
    sibling = (tm, space + 1 - 2 * core)
    partner = (tm + 1 - 2 * slot, space)
    opposite = (3 - tm, space)

    def on_y(d):
        p = lax.rem(y + d, 8)
        return p, (tm, (z * 8 + p) * 2 + core)

    def on_z(d):
        p = lax.rem(z + d, 8)
        return p, (tm, (p * 8 + y) * 2 + core)

    def on_x(d):
        return lax.rem(tm + d, 4), (lax.rem(tm + d, 4), space)

    first_axis, second_axis = (on_y, on_z), (on_z, on_y)
    first_at, second_at = (y, z), (z, y)
    others = [sibling] + [on_x(d)[1] for d in range(1, 4)]
    for d in range(1, 8):
        others += [on_y(d)[1], on_z(d)[1]]
    enter(others)

    to_partner = remote(own_ref, stacked_ref.at[slot], x_sem, (0,), partner)
    to_opposite = remote(own_ref, across, x_sem, (1,), opposite)
    stacked_ref[slot] = own_ref[...]
    to_partner.wait()

    tn = ((0,), (0,))
    low, high = stacked_ref[0], stacked_ref[1]
    for base, block in ((0, (low, low)), (3, (high, high)), (6, (low, high))):
        g = bf_dot(block[0], block[1], tn)
        places = ((0, 0), (1, 0), (1, 1)) if base < 6 else ((0, 0), (0, 1), (1, 0), (1, 1))
        for i, (r, c) in enumerate(places):
            block = g[H * r : H * r + H, H * c : H * c + H]
            store_pieces(part, block, H * (base + i), PAIR_ROWS, 0)
    to_opposite.wait()
    first_pair = tm < 2
    left = jnp.where(first_pair, own_ref[...], across[...])
    right = jnp.where(first_pair, across[...], stacked_ref[1 - slot])
    g = bf_dot(left, right, tn)
    for i, (r, c) in enumerate(((0, 0), (0, 1), (1, 0), (1, 1))):
        block = g[H * r : H * r + H, H * c : H * c + H]
        store_pieces(part, block, H * i, CROSS_ROWS, PAIR_ROWS)

    remote(part.at[span((1 - core) * HALF, HALF)], recv0, core_sem, (0,), sibling).wait()
    half[...] = part[span(core * HALF, HALF), :] + recv0[...]

    copies = []
    for d in FAR_FIRST:
        for h in range(2):
            p, device = first_axis[h](d)
            source = half.at[span(h * QUARTER + p * CHUNK, CHUNK)]
            copies.append(remote(source, recv1.at[h, first_at[h]], sem1, (h, d), device))
    for h in range(2):
        recv1[h, first_at[h]] = half[span(h * QUARTER + first_at[h] * CHUNK, CHUNK), :]
    for copy in copies:
        copy.wait()
    for h in range(2):
        total = recv1[h, 0]
        for p in range(1, 8):
            total = total + recv1[h, p]
        sum1[h] = total

    copies = []
    for d in FAR_FIRST:
        for h in range(2):
            device = second_axis[h](d)[1]
            copies.append(remote(sum1.at[h], recv2.at[h, second_at[h]], sem2, (h, d), device))
    for h in range(2):
        recv2[h, second_at[h]] = sum1[h]
    for copy in copies:
        copy.wait()

    def chunk(h, p):
        return core * (CHUNKS // 2) + h * (CHUNKS // 4) + p

    def pair_at(h, p):
        return packed_ref.at[span(chunk(h, p) * PAIR_ROWS, PAIR_ROWS)]

    def cross_at(h, p):
        return cross_ref.at[span(chunk(h, p) * 4 * CROSS_ROWS, 4 * CROSS_ROWS)]

    def plane_at(h, plane):
        start = (chunk(h, first_at[h]) * 4 + plane) * CROSS_ROWS
        return cross_ref.at[span(start, CROSS_ROWS)]

    for h in range(2):
        total = recv2[h, 0]
        for p in range(1, 8):
            total = total + recv2[h, p]
        pair_at(h, first_at[h])[...] = total[:PAIR_ROWS]
        plane_at(h, tm)[...] = total[PAIR_ROWS:]

    along_x, pairs, crosses, forwards = [], [], [], []
    for d in range(1, 4):
        for h in range(2):
            mine = plane_at(h, tm)
            along_x.append(remote(mine, mine, sem_x, (h, d), on_x(d)[1]))
    for d in FAR_FIRST:
        for h in range(2):
            mine = pair_at(h, first_at[h])
            pairs.append((h, d, remote(mine, mine, sem_pair, (h, d), first_axis[h](d)[1])))
    for h in range(2):
        mine = pair_at(h, first_at[h])
        forwards.append(remote(mine, mine, sem_pair_core, (h, 0), sibling))
    for copy in along_x:
        copy.wait()
    for d in FAR_FIRST:
        for h in range(2):
            mine = cross_at(h, first_at[h])
            crosses.append((h, d, remote(mine, mine, sem_cross, (h, d), first_axis[h](d)[1])))
    for h in range(2):
        mine = cross_at(h, first_at[h])
        forwards.append(remote(mine, mine, sem_cross_core, (h, 0), sibling))
    for copies, at, sems in ((pairs, pair_at, sem_pair_core), (crosses, cross_at, sem_cross_core)):
        for h, d, copy in copies[::-1]:
            copy.wait()
            arrived = at(h, lax.rem(first_at[h] + 8 - d, 8))
            forwards.append(remote(arrived, arrived, sems, (h, d), sibling))
    for copy in forwards:
        copy.wait()


def gram(own):
    dma = pltpu.SemaphoreType.DMA
    vmem = pl.BlockSpec(memory_space=pltpu.VMEM)
    return pl.pallas_call(
        gram_kernel,
        out_shape=(
            jax.ShapeDtypeStruct((PAIR, H), F32),
            jax.ShapeDtypeStruct((4 * CROSS, H), F32),
            jax.ShapeDtypeStruct((2, 256, K), BF16),
        ),
        in_specs=[vmem],
        out_specs=[vmem] * 3,
        scratch_shapes=[
            pltpu.VMEM((256, K), BF16),
            pltpu.VMEM((ROWS, H), F32),
            pltpu.VMEM((HALF, H), F32),
            pltpu.VMEM((HALF, H), F32),
            pltpu.VMEM((2, 8, CHUNK, H), F32),
            pltpu.VMEM((2, CHUNK, H), F32),
            pltpu.VMEM((2, 8, CHUNK, H), F32),
            dma((2, 2)),
            dma((2, 1)),
            dma((2, 2, 8)),
            dma((2, 2, 8)),
            dma((2, 2, 8)),
            dma((2, 2, 8)),
            dma((2, 2, 4)),
            dma((2, 2, 8)),
            dma((2, 2, 8)),
        ],
        compiler_params=pltpu.CompilerParams(
            collective_id=0, has_side_effects=True, vmem_limit_bytes=VMEM_LIMIT
        ),
        name="gram_all",
    )(own)


def swap_kernel(rot_ref, own_ref, diag_ref, rots_ref, rows_ref, diags_ref, sem, core_sem):
    tm, space = lax.axis_index("tm"), lax.axis_index("space")
    core, slot = lax.rem(space, 2), lax.div(tm, 2)
    sibling = (tm, space + 1 - 2 * core)
    opposite = (3 - tm, space)
    enter([sibling, opposite])

    rot_rows, diag_rows = K // 2, 3 * H // 2
    rot_part = pl.ds(pl.multiple_of(core * rot_rows, 16), rot_rows)
    diag_part = span(core * diag_rows, diag_rows)
    rots = remote(rot_ref.at[rot_part], rots_ref.at[slot, rot_part], sem, (0,), opposite)
    diags = remote(diag_ref.at[diag_part], diags_ref.at[slot, diag_part], sem, (1,), opposite)
    rows = remote(own_ref, rows_ref.at[slot], sem, (2,), opposite)
    rots_ref[slot] = rot_ref[...]
    diags_ref[slot] = diag_ref[...]
    rows_ref[slot] = own_ref[...]
    rots.wait()
    arrived = rots_ref.at[1 - slot, rot_part]
    rots = remote(arrived, arrived, core_sem, (0,), sibling)
    diags.wait()
    arrived = diags_ref.at[1 - slot, diag_part]
    diags = remote(arrived, arrived, core_sem, (1,), sibling)
    for copy in (rows, rots, diags):
        copy.wait()


def swap(rot, own, diag):
    vmem = pl.BlockSpec(memory_space=pltpu.VMEM)
    return pl.pallas_call(
        swap_kernel,
        out_shape=tuple(jax.ShapeDtypeStruct((2,) + a.shape, a.dtype) for a in (rot, own, diag)),
        in_specs=[vmem] * 3,
        out_specs=[vmem] * 3,
        scratch_shapes=[pltpu.SemaphoreType.DMA((2, 3)), pltpu.SemaphoreType.DMA((2, 2))],
        compiler_params=pltpu.CompilerParams(
            collective_id=1, has_side_effects=True, vmem_limit_bytes=VMEM_LIMIT
        ),
        name="swap_rotations",
    )(rot, own, diag)


def body(bases):
    packed, cross, stacked = gram(bases[0])
    rots, rows, diags = swap(*merge_pair(packed, stacked))
    return merge_last(cross, rots, rows, diags)


def solution(mesh):
    return jax.shard_map(
        body,
        mesh=mesh,
        in_specs=(P("tm", "space", None),),
        out_specs=P("space", "tm"),
        check_vma=False,
    )
```

```python
import functools

import jax
import jax.numpy as jnp
from jax import lax
from jax.experimental import pallas as pl
from jax.experimental.pallas import tpu as pltpu
from jax.sharding import PartitionSpec as P

MESH = pl.DeviceIdType.MESH
F32 = jnp.float32
BF16 = jnp.bfloat16
K = 256
H = 128
GRID = 32768
PAIR_ROWS = 40
CROSS_ROWS = 16
CHUNK = PAIR_ROWS + CROSS_ROWS
CHUNKS = 32
PAIR = PAIR_ROWS * CHUNKS
CROSS = CROSS_ROWS * CHUNKS
ROWS = CHUNK * CHUNKS
QUARTER = ROWS // 4
HALF = ROWS // 2
FAR_FIRST = (4, 3, 5, 2, 6, 1, 7)
VMEM_LIMIT = 48 * 1024 * 1024


def dot(a, b, dims=((1,), (0,))):
    return lax.dot_general(
        a,
        b,
        (dims, ((), ())),
        precision=lax.Precision.HIGHEST,
        preferred_element_type=F32,
    )


def dot_nt(a, b):
    return dot(a, b, ((1,), (1,)))


def dot_tn(a, b):
    return dot(a, b, ((0,), (0,)))


def lane_bc(x, c):
    return jnp.broadcast_to(x[:, c : c + 1], x.shape)


def sub_bc(x, r):
    return jnp.broadcast_to(x[r : r + 1, :], x.shape)


def weighted(cols, rows):
    s0 = cols[0] * rows[0]
    s1 = cols[1] * rows[1]
    for c in range(2, 8, 2):
        s0 = s0 + cols[c] * rows[c]
        s1 = s1 + cols[c + 1] * rows[c + 1]
    return s0 + s1


def factor_block(w, offset):
    groups = 8
    sub = lax.broadcasted_iota(jnp.int32, (8, 128), 0)
    rows = [w[8 * g : 8 * g + 8] for g in range(groups)]
    done = []
    pending = []

    def spread(h, g):
        return [lane_bc(rows[h], offset + 8 * g + c) for c in range(8)]

    def update(h, cols, v):
        rows[h] = rows[h] - weighted(cols, v)

    p = spread(0, 0)
    below, ahead = spread(1, 0), spread(1, 1)
    later = {h: spread(h, 0) for h in range(2, groups)}
    for g in range(groups):
        jordan = forward = rows[g]
        recips = jnp.ones_like(jordan)
        last = g == groups - 1
        raw = list(below)
        for j in range(8):
            r = 1.0 / sub_bc(p[j], j)
            f = p[j] * r
            f_all = jnp.where(sub != j, f, 0.0)
            if not last:
                f_next = below[j] * r
                row_next = [sub_bc(below[j], c) for c in range(8)]
            for c in range(j + 1, 8):
                row = sub_bc(p[c], j)
                p[c] = p[c] - f_all * row
                if not last:
                    below[c] = below[c] - f_next * row
            if not last:
                ahead = [a - f_next * x for a, x in zip(ahead, row_next)]
            x = sub_bc(jordan, j)
            jordan = jordan - f_all * x
            if j < 7:
                forward = forward - jnp.where(sub > j, f, 0.0) * x
            recips = jnp.where(sub == j, r, recips)
            if pending:
                pending.pop(0)()
            yield None
        while pending:
            pending.pop(0)()
        done.append(forward * jnp.sqrt(recips))
        if last:
            break
        v = jordan * recips
        v = [sub_bc(v, c) for c in range(8)]
        p = ahead
        if g + 2 < groups:
            update(g + 2, later.pop(g + 2), v)
            below, ahead = spread(g + 2, g + 1), spread(g + 2, g + 2)
        update(g + 1, raw, v)

        def finish(h, g=g, v=v):
            update(h, later.pop(h), v)
            later[h] = spread(h, g + 1)

        pending = [functools.partial(finish, h) for h in range(g + 3, groups)]
    return jnp.concatenate(done, 0)


def cholesky_128(a):
    half = H // 2
    row = lax.broadcasted_iota(jnp.int32, (half, H), 0)
    lane = lax.broadcasted_iota(jnp.int32, (half, H), 1)
    low = lane < half
    one, zero = jnp.ones((half, H), F32), jnp.zeros((half, H), F32)
    top, bottom = a[:half], a[half:]
    w = jnp.where(low, top, jnp.where(lane == row + half, one, zero))
    f1 = yield from factor_block(w, 0)
    inv1 = pltpu.roll(jnp.where(low, 0.0, f1), half, 1)
    l21 = dot_nt(bottom, inv1)
    yield
    rest = bottom - dot_nt(l21, jnp.concatenate([jnp.zeros((half, half), F32), l21], 0))
    w = jnp.where(low, jnp.where(lane == row, one, zero), rest)
    yield
    q = dot(l21, inv1)
    u1 = dot(inv1[:, :half], top)
    f2 = yield from factor_block(w, half)
    inv2 = jnp.where(low, f2, 0.0)
    x = dot(inv2[:, :half], q)
    inverse = jnp.concatenate([inv1, pltpu.roll(inv2, half, 1) - x], 0)
    upper = jnp.concatenate(
        [jnp.where(lane >= row, u1, 0.0), jnp.where(lane >= row + half, f2, 0.0)], 0
    )
    return upper, inverse


def together(*steps):
    results = [None] * len(steps)
    running = list(enumerate(steps))
    while running:
        for item in list(running):
            try:
                next(item[1])
            except StopIteration as end:
                results[item[0]] = end.value
                running.remove(item)
        yield
    return results


def run_together(*steps):
    work = together(*steps)
    while True:
        try:
            next(work)
        except StopIteration as end:
            return end.value


def split3(x):
    hi = x.astype(BF16)
    rest = x - hi.astype(F32)
    mid = rest.astype(BF16)
    low = (rest - mid.astype(F32)).astype(BF16)
    return hi, mid, low


def bf_dot(a, b, dims=((1,), (0,))):
    return lax.dot_general(a, b, (dims, ((), ())), preferred_element_type=F32)


def rounded_left(a, x):
    hi, mid, low = split3(x)
    return bf_dot(a, low) + bf_dot(a, mid) + bf_dot(a, hi)


def rounded_right_nt(x, a):
    nt = ((1,), (1,))
    hi, mid, low = split3(x)
    return bf_dot(low, a, nt) + bf_dot(mid, a, nt) + bf_dot(hi, a, nt)


def put(ref, r, c, block):
    ref[H * r : H * r + H, H * c : H * c + H] = block


def unpack_pair(packed_ref, gram_ref):
    b = [packed_ref[H * i : H * i + H, :] * (1.0 / GRID) for i in range(10)]
    for base, at in ((0, 0), (3, 2)):
        put(gram_ref, at, at, b[base])
        put(gram_ref, at + 1, at, b[base + 1])
        put(gram_ref, at, at + 1, b[base + 1].T)
        put(gram_ref, at + 1, at + 1, b[base + 2])
    for i, (r, c) in enumerate(((0, 2), (0, 3), (1, 2), (1, 3))):
        put(gram_ref, r, c, b[6 + i])
        put(gram_ref, c, r, b[6 + i].T)


CROSS_AT = ((0, 1), (1, 0), (1, 1), (0, 0))


def unpack_cross(cross_ref, gram_ref):
    for plane, (r, c) in enumerate(CROSS_AT):
        for i, (rr, cc) in enumerate(((0, 0), (0, 1), (1, 0), (1, 1))):
            for k in range(H // CROSS_ROWS):
                chunk = i * (H // CROSS_ROWS) + k
                at = (chunk * 4 + plane) * CROSS_ROWS
                top, left = K * r + H * rr + CROSS_ROWS * k, K * c + H * cc
                gram_ref[top : top + CROSS_ROWS, left : left + H] = cross_ref[
                    at : at + CROSS_ROWS, :
                ] * (1.0 / GRID)


def rotation_transposed(gram_ref):
    gram = gram_ref[...]
    y1 = gram[:K] + gram[K:]
    y1t, y1b = y1[:H], y1[H:]
    z1t = dot(y1t, gram)
    m11 = dot_nt(y1t, z1t)

    def metric_rest():
        z1b = dot(y1b, gram)
        yield
        m21 = dot_nt(y1b, z1t)
        yield
        return z1b, m21, dot_nt(y1b, z1b)

    (_, inv1), (z1b, m21, m22) = run_together(cholesky_128(m11), metric_rest())

    y2t = dot(inv1, z1t)

    def first_factor_rest():
        l21 = dot_nt(m21, inv1)
        yield
        _, inv2 = yield from cholesky_128(m22 - dot_nt(l21, l21))
        y2b = dot(inv2, z1b - dot(l21, y2t))
        yield
        return y2b, dot(y2b, gram)

    def second_factors():
        a2t = dot(y2t, gram)
        yield
        p11, e11 = dot_nt(y2t, a2t), dot_nt(a2t, a2t)
        yield
        factors = yield from together(cholesky_128(p11), cholesky_128(e11))
        return a2t, factors

    (y2b, a2b), (a2t, ((_, p_inv1), (e_up1, e_inv1))) = run_together(
        first_factor_rest(), second_factors()
    )
    p_l21 = dot_nt(dot_nt(y2b, a2t), p_inv1)
    e_l21 = dot_nt(dot_nt(a2b, a2t), e_inv1)
    p_rest = dot_nt(y2b, a2b) - dot_nt(p_l21, p_l21)
    e_rest = dot_nt(a2b, a2b) - dot_nt(e_l21, e_l21)

    def frame_top():
        f2t = dot(p_inv1, y2t)
        yield
        solved = y2b - dot(p_l21, f2t)
        yield
        s11 = dot_nt(e_up1, p_inv1)
        yield
        e_u12 = dot(e_inv1, dot_nt(a2t, a2b))
        yield
        s_rest = e_u12 - dot_nt(s11, p_l21)
        yield
        return solved, s_rest, dot(s11, f2t)

    (_, p_inv2), (e_up2, _), (solved, s_rest, rot_top) = run_together(
        cholesky_128(p_rest), cholesky_128(e_rest), frame_top()
    )
    f2b = dot(p_inv2, solved)
    rot_top = rot_top + dot(dot_nt(s_rest, p_inv2), f2b)
    rot_bottom = dot(dot_nt(e_up2, p_inv2), f2b)
    return jnp.concatenate([rot_top, rot_bottom], 0).astype(BF16)


def merge_last_kernel(cross_ref, rots_ref, rows_ref, diags_ref, out_ref, gram_ref, rot_ref):
    unpack_cross(cross_ref, gram_ref)
    cross = rounded_right_nt(rounded_left(rots_ref[0], gram_ref[...]), rots_ref[1])
    gram_ref[:K, K:] = cross
    gram_ref[K:, :K] = cross.T
    for i in range(2):
        b = [diags_ref[i, H * k : H * k + H, :] for k in range(3)]
        put(gram_ref, 2 * i, 2 * i, b[0])
        put(gram_ref, 2 * i + 1, 2 * i, b[1])
        put(gram_ref, 2 * i, 2 * i + 1, b[1].T)
        put(gram_ref, 2 * i + 1, 2 * i + 1, b[2])
    rot_ref[...] = rotation_transposed(gram_ref)
    width = out_ref.shape[1]
    start = pl.multiple_of(lax.axis_index("tm") * width, width)
    rot = rot_ref[pl.ds(start, width), :]
    nt = ((1,), (1,))
    out_ref[...] = bf_dot(rows_ref[0], rot[:, :K], nt) + bf_dot(rows_ref[1], rot[:, K:], nt)


def merge_last(cross, rots, rows, diags):
    vmem = pl.BlockSpec(memory_space=pltpu.VMEM)
    return pl.pallas_call(
        merge_last_kernel,
        out_shape=jax.ShapeDtypeStruct((256, 64), F32),
        in_specs=[vmem] * 4,
        out_specs=vmem,
        scratch_shapes=[pltpu.VMEM((2 * K, 2 * K), F32), pltpu.VMEM((K, 2 * K), BF16)],
        compiler_params=pltpu.CompilerParams(vmem_limit_bytes=VMEM_LIMIT),
        name="merge_last",
    )(cross, rots, rows, diags)


def enter(devices):
    barrier = pltpu.get_barrier_semaphore()
    for device in devices:
        pl.semaphore_signal(barrier, inc=1, device_id=device, device_id_type=MESH)
    pl.semaphore_wait(barrier, len(devices))


def remote(src, dst, sems, index, device):
    copy = pltpu.make_async_remote_copy(
        src_ref=src,
        dst_ref=dst,
        send_sem=sems.at[(0,) + index],
        recv_sem=sems.at[(1,) + index],
        device_id=device,
        device_id_type=MESH,
    )
    copy.start()
    return copy


def span(start, count):
    return pl.ds(pl.multiple_of(start, 8), count)


def store_pieces(part, block, first, per_chunk, offset):
    row = 0
    while row < block.shape[0]:
        chunk, at = divmod(first + row, per_chunk)
        count = min(per_chunk - at, block.shape[0] - row)
        to = chunk * CHUNK + offset + at
        part[to : to + count, :] = block[row : row + count]
        row += count


def first_level_kernel(
    own_ref, cross_ref, rots_ref, rows_ref, diags_ref, packed_ref, stacked_ref, gram_ref,
    across, part, half, recv0, recv1, sum1, recv2,
    x_sem, core_sem, sem1, sem2, sem_pair, sem_pair_core, sem_x, sem_cross, sem_cross_core,
    sem_swap, sem_swap_core,
):
    tm, space = lax.axis_index("tm"), lax.axis_index("space")
    core, y, z = lax.rem(space, 2), lax.rem(lax.div(space, 2), 8), lax.div(space, 16)
    slot = lax.rem(tm, 2)
    sibling = (tm, space + 1 - 2 * core)
    partner = (tm + 1 - 2 * slot, space)
    opposite = (3 - tm, space)

    def on_y(d):
        p = lax.rem(y + d, 8)
        return p, (tm, (z * 8 + p) * 2 + core)

    def on_z(d):
        p = lax.rem(z + d, 8)
        return p, (tm, (p * 8 + y) * 2 + core)

    def on_x(d):
        return lax.rem(tm + d, 4), (lax.rem(tm + d, 4), space)

    first_axis, second_axis = (on_y, on_z), (on_z, on_y)
    first_at, second_at = (y, z), (z, y)
    others = [sibling] + [on_x(d)[1] for d in range(1, 4)]
    for d in range(1, 8):
        others += [on_y(d)[1], on_z(d)[1]]
    enter(others)

    to_partner = remote(own_ref, stacked_ref.at[slot], x_sem, (0,), partner)
    to_opposite = remote(own_ref, across, x_sem, (1,), opposite)
    stacked_ref[slot] = own_ref[...]
    to_partner.wait()

    tn = ((0,), (0,))
    low, high = stacked_ref[0], stacked_ref[1]
    for base, block in ((0, (low, low)), (3, (high, high)), (6, (low, high))):
        g = bf_dot(block[0], block[1], tn)
        places = ((0, 0), (1, 0), (1, 1)) if base < 6 else ((0, 0), (0, 1), (1, 0), (1, 1))
        for i, (r, c) in enumerate(places):
            block = g[H * r : H * r + H, H * c : H * c + H]
            store_pieces(part, block, H * (base + i), PAIR_ROWS, 0)
    to_opposite.wait()
    first_pair = tm < 2
    left = jnp.where(first_pair, own_ref[...], across[...])
    right = jnp.where(first_pair, across[...], stacked_ref[1 - slot])
    g = bf_dot(left, right, tn)
    for i, (r, c) in enumerate(((0, 0), (0, 1), (1, 0), (1, 1))):
        block = g[H * r : H * r + H, H * c : H * c + H]
        store_pieces(part, block, H * i, CROSS_ROWS, PAIR_ROWS)

    def in_half(h, p):
        return span(h * QUARTER + p * CHUNK, CHUNK)

    order = [(h, d) for d in FAR_FIRST + (0,) for h in range(2)]
    halves, copies = [], []
    for h, d in order:
        p = lax.rem(first_at[h] + d, 8)
        theirs = part.at[span((1 - core) * HALF + h * QUARTER + p * CHUNK, CHUNK)]
        halves.append(remote(theirs, recv0.at[in_half(h, p)], core_sem, (h, d), sibling))
    for (h, d), copy in zip(order, halves):
        copy.wait()
        p = lax.rem(first_at[h] + d, 8)
        mine = span(core * HALF + h * QUARTER + p * CHUNK, CHUNK)
        total = part[mine, :] + recv0[in_half(h, p), :]
        if d:
            half[in_half(h, p), :] = total
            to = first_axis[h](d)[1]
            copies.append(remote(half.at[in_half(h, p)], recv1.at[h, first_at[h]], sem1, (h, d), to))
        else:
            recv1[h, p] = total
    for copy in copies:
        copy.wait()
    for h in range(2):
        total = recv1[h, 0]
        for p in range(1, 8):
            total = total + recv1[h, p]
        sum1[h] = total

    copies = []
    for d in FAR_FIRST:
        for h in range(2):
            device = second_axis[h](d)[1]
            copies.append(remote(sum1.at[h], recv2.at[h, second_at[h]], sem2, (h, d), device))
    for h in range(2):
        recv2[h, second_at[h]] = sum1[h]
    for copy in copies:
        copy.wait()

    def chunk(h, p):
        return core * (CHUNKS // 2) + h * (CHUNKS // 4) + p

    def pair_at(h, p):
        return packed_ref.at[span(chunk(h, p) * PAIR_ROWS, PAIR_ROWS)]

    def cross_at(h, p):
        return cross_ref.at[span(chunk(h, p) * 4 * CROSS_ROWS, 4 * CROSS_ROWS)]

    def plane_at(h, plane):
        start = (chunk(h, first_at[h]) * 4 + plane) * CROSS_ROWS
        return cross_ref.at[span(start, CROSS_ROWS)]

    for h in range(2):
        total = recv2[h, 0]
        for p in range(1, 8):
            total = total + recv2[h, p]
        pair_at(h, first_at[h])[...] = total[:PAIR_ROWS]
        plane_at(h, tm)[...] = total[PAIR_ROWS:]

    along_x, pairs, crosses, forwards = [], [], [], []
    for d in range(1, 4):
        for h in range(2):
            mine = plane_at(h, tm)
            along_x.append(remote(mine, mine, sem_x, (h, d), on_x(d)[1]))
    for d in FAR_FIRST:
        for h in range(2):
            mine = pair_at(h, first_at[h])
            pairs.append((h, d, remote(mine, mine, sem_pair, (h, d), first_axis[h](d)[1])))
    for h in range(2):
        mine = pair_at(h, first_at[h])
        forwards.append(remote(mine, mine, sem_pair_core, (h, 0), sibling))
    for copy in along_x:
        copy.wait()
    for d in FAR_FIRST:
        for h in range(2):
            mine = cross_at(h, first_at[h])
            crosses.append((h, d, remote(mine, mine, sem_cross, (h, d), first_axis[h](d)[1])))

    def forward(copies, at, sems):
        for h, d, copy in copies[::-1]:
            copy.wait()
            arrived = at(h, lax.rem(first_at[h] + 8 - d, 8))
            forwards.append(remote(arrived, arrived, sems, (h, d), sibling))
        for copy in forwards:
            copy.wait()

    forward(pairs, pair_at, sem_pair_core)

    unpack_pair(packed_ref, gram_ref)
    rot = rotation_transposed(gram_ref)
    side = lax.div(tm, 2)
    rot_rows, diag_rows = K // 2, 3 * H // 2
    rot_part = pl.ds(pl.multiple_of(core * rot_rows, 16), rot_rows)
    diag_part = span(core * diag_rows, diag_rows)
    rots_ref[side] = rot
    mine = rots_ref.at[side, rot_part]
    swap_rots = remote(mine, mine, sem_swap, (0,), opposite)
    forwards = []
    for h in range(2):
        mine = cross_at(h, first_at[h])
        forwards.append(remote(mine, mine, sem_cross_core, (h, 0), sibling))
    nt = ((1,), (1,))
    rows_ref[side] = (
        bf_dot(stacked_ref[0], rot[:, :K], nt) + bf_dot(stacked_ref[1], rot[:, K:], nt)
    ).astype(BF16)
    mine = rows_ref.at[side]
    swap_rows = remote(mine, mine, sem_swap, (1,), opposite)
    diag = rounded_right_nt(rounded_left(rot, gram_ref[...]), rot)
    for i, (r, c) in enumerate(((0, 0), (1, 0), (1, 1))):
        diags_ref[side, H * i : H * i + H, :] = diag[H * r : H * r + H, H * c : H * c + H]
    mine = diags_ref.at[side, diag_part]
    swap_diags = remote(mine, mine, sem_swap, (2,), opposite)
    forward(crosses, cross_at, sem_cross_core)
    swap_rots.wait()
    arrived = rots_ref.at[1 - side, rot_part]
    share_rots = remote(arrived, arrived, sem_swap_core, (0,), sibling)
    swap_diags.wait()
    arrived = diags_ref.at[1 - side, diag_part]
    share_diags = remote(arrived, arrived, sem_swap_core, (1,), sibling)
    for copy in (swap_rows, share_rots, share_diags):
        copy.wait()


def first_level(own):
    dma = pltpu.SemaphoreType.DMA
    vmem = pl.BlockSpec(memory_space=pltpu.VMEM)
    return pl.pallas_call(
        first_level_kernel,
        out_shape=(
            jax.ShapeDtypeStruct((4 * CROSS, H), F32),
            jax.ShapeDtypeStruct((2, K, 2 * K), BF16),
            jax.ShapeDtypeStruct((2, 256, K), BF16),
            jax.ShapeDtypeStruct((2, 3 * H, H), F32),
        ),
        in_specs=[vmem],
        out_specs=[vmem] * 4,
        scratch_shapes=[
            pltpu.VMEM((PAIR, H), F32),
            pltpu.VMEM((2, 256, K), BF16),
            pltpu.VMEM((2 * K, 2 * K), F32),
            pltpu.VMEM((256, K), BF16),
            pltpu.VMEM((ROWS, H), F32),
            pltpu.VMEM((HALF, H), F32),
            pltpu.VMEM((HALF, H), F32),
            pltpu.VMEM((2, 8, CHUNK, H), F32),
            pltpu.VMEM((2, CHUNK, H), F32),
            pltpu.VMEM((2, 8, CHUNK, H), F32),
            dma((2, 2)),
            dma((2, 2, 8)),
            dma((2, 2, 8)),
            dma((2, 2, 8)),
            dma((2, 2, 8)),
            dma((2, 2, 8)),
            dma((2, 2, 4)),
            dma((2, 2, 8)),
            dma((2, 2, 8)),
            dma((2, 3)),
            dma((2, 2)),
        ],
        compiler_params=pltpu.CompilerParams(
            collective_id=0, has_side_effects=True, vmem_limit_bytes=VMEM_LIMIT
        ),
        name="first_level",
    )(own)


def body(bases):
    return merge_last(*first_level(bases[0]))


def solution(mesh):
    return jax.shard_map(
        body,
        mesh=mesh,
        in_specs=(P("tm", "space", None),),
        out_specs=P("space", "tm"),
        check_vma=False,
    )
```

```python
import functools

import jax
import jax.numpy as jnp
from jax import lax
from jax.experimental import pallas as pl
from jax.experimental.pallas import tpu as pltpu
from jax.sharding import PartitionSpec as P

MESH = pl.DeviceIdType.MESH
F32 = jnp.float32
BF16 = jnp.bfloat16
K = 256
H = 128
GRID = 32768
PAIR_ROWS = 40
CROSS_ROWS = 16
CHUNK = PAIR_ROWS + CROSS_ROWS
CHUNKS = 32
PAIR = PAIR_ROWS * CHUNKS
CROSS = CROSS_ROWS * CHUNKS
ROWS = CHUNK * CHUNKS
QUARTER = ROWS // 4
HALF = ROWS // 2
SWAP_PIECES = 4
FAR_FIRST = (4, 3, 5, 2, 6, 1, 7)
VMEM_LIMIT = 48 * 1024 * 1024


def dot(a, b, dims=((1,), (0,))):
    return lax.dot_general(
        a,
        b,
        (dims, ((), ())),
        precision=lax.Precision.HIGHEST,
        preferred_element_type=F32,
    )


def dot_nt(a, b):
    return dot(a, b, ((1,), (1,)))


def dot_tn(a, b):
    return dot(a, b, ((0,), (0,)))


def lane_bc(x, c):
    return jnp.broadcast_to(x[:, c : c + 1], x.shape)


def sub_bc(x, r):
    return jnp.broadcast_to(x[r : r + 1, :], x.shape)


def weighted(cols, rows):
    s0 = cols[0] * rows[0]
    s1 = cols[1] * rows[1]
    for c in range(2, 8, 2):
        s0 = s0 + cols[c] * rows[c]
        s1 = s1 + cols[c + 1] * rows[c + 1]
    return s0 + s1


def factor_block(w, offset):
    groups = 8
    sub = lax.broadcasted_iota(jnp.int32, (8, 128), 0)
    rows = [w[8 * g : 8 * g + 8] for g in range(groups)]
    done = []
    pending = []

    def spread(h, g):
        return [lane_bc(rows[h], offset + 8 * g + c) for c in range(8)]

    def update(h, cols, v):
        rows[h] = rows[h] - weighted(cols, v)

    p = spread(0, 0)
    below, ahead = spread(1, 0), spread(1, 1)
    later = {h: spread(h, 0) for h in range(2, groups)}
    for g in range(groups):
        jordan = forward = rows[g]
        recips = jnp.ones_like(jordan)
        last = g == groups - 1
        raw = list(below)
        for j in range(8):
            r = 1.0 / sub_bc(p[j], j)
            f = p[j] * r
            f_all = jnp.where(sub != j, f, 0.0)
            if not last:
                f_next = below[j] * r
                row_next = [sub_bc(below[j], c) for c in range(8)]
            for c in range(j + 1, 8):
                row = sub_bc(p[c], j)
                p[c] = p[c] - f_all * row
                if not last:
                    below[c] = below[c] - f_next * row
            if not last:
                ahead = [a - f_next * x for a, x in zip(ahead, row_next)]
            x = sub_bc(jordan, j)
            jordan = jordan - f_all * x
            if j < 7:
                forward = forward - jnp.where(sub > j, f, 0.0) * x
            recips = jnp.where(sub == j, r, recips)
            if pending:
                pending.pop(0)()
            yield None
        while pending:
            pending.pop(0)()
        done.append(forward * jnp.sqrt(recips))
        if last:
            break
        v = jordan * recips
        v = [sub_bc(v, c) for c in range(8)]
        p = ahead
        if g + 2 < groups:
            update(g + 2, later.pop(g + 2), v)
            below, ahead = spread(g + 2, g + 1), spread(g + 2, g + 2)
        update(g + 1, raw, v)

        def finish(h, g=g, v=v):
            update(h, later.pop(h), v)
            later[h] = spread(h, g + 1)

        pending = [functools.partial(finish, h) for h in range(g + 3, groups)]
    return jnp.concatenate(done, 0)


def cholesky_128(a):
    half = H // 2
    row = lax.broadcasted_iota(jnp.int32, (half, H), 0)
    lane = lax.broadcasted_iota(jnp.int32, (half, H), 1)
    low = lane < half
    one, zero = jnp.ones((half, H), F32), jnp.zeros((half, H), F32)
    top, bottom = a[:half], a[half:]
    w = jnp.where(low, top, jnp.where(lane == row + half, one, zero))
    f1 = yield from factor_block(w, 0)
    inv1 = pltpu.roll(jnp.where(low, 0.0, f1), half, 1)
    l21 = dot_nt(bottom, inv1)
    yield
    rest = bottom - dot_nt(l21, jnp.concatenate([jnp.zeros((half, half), F32), l21], 0))
    w = jnp.where(low, jnp.where(lane == row, one, zero), rest)
    yield
    q = dot(l21, inv1)
    u1 = dot(inv1[:, :half], top)
    f2 = yield from factor_block(w, half)
    inv2 = jnp.where(low, f2, 0.0)
    x = dot(inv2[:, :half], q)
    inverse = jnp.concatenate([inv1, pltpu.roll(inv2, half, 1) - x], 0)
    upper = jnp.concatenate(
        [jnp.where(lane >= row, u1, 0.0), jnp.where(lane >= row + half, f2, 0.0)], 0
    )
    return upper, inverse


def together(*steps):
    results = [None] * len(steps)
    running = list(enumerate(steps))
    while running:
        for item in list(running):
            try:
                next(item[1])
            except StopIteration as end:
                results[item[0]] = end.value
                running.remove(item)
        yield
    return results


def run_together(*steps):
    work = together(*steps)
    while True:
        try:
            next(work)
        except StopIteration as end:
            return end.value


def split3(x):
    hi = x.astype(BF16)
    rest = x - hi.astype(F32)
    mid = rest.astype(BF16)
    low = (rest - mid.astype(F32)).astype(BF16)
    return hi, mid, low


def bf_dot(a, b, dims=((1,), (0,))):
    return lax.dot_general(a, b, (dims, ((), ())), preferred_element_type=F32)


def rounded_left(a, x):
    hi, mid, low = split3(x)
    return bf_dot(a, low) + bf_dot(a, mid) + bf_dot(a, hi)


def rounded_right_nt(x, a):
    nt = ((1,), (1,))
    hi, mid, low = split3(x)
    return bf_dot(low, a, nt) + bf_dot(mid, a, nt) + bf_dot(hi, a, nt)


def put(ref, r, c, block):
    ref[H * r : H * r + H, H * c : H * c + H] = block


def unpack_pair(packed_ref, gram_ref):
    b = [packed_ref[H * i : H * i + H, :] * (1.0 / GRID) for i in range(10)]
    for base, at in ((0, 0), (3, 2)):
        put(gram_ref, at, at, b[base])
        put(gram_ref, at + 1, at, b[base + 1])
        put(gram_ref, at, at + 1, b[base + 1].T)
        put(gram_ref, at + 1, at + 1, b[base + 2])
    for i, (r, c) in enumerate(((0, 2), (0, 3), (1, 2), (1, 3))):
        put(gram_ref, r, c, b[6 + i])
        put(gram_ref, c, r, b[6 + i].T)


CROSS_AT = ((0, 1), (1, 0), (1, 1), (0, 0))


def unpack_cross(cross_ref, gram_ref):
    for plane, (r, c) in enumerate(CROSS_AT):
        for i, (rr, cc) in enumerate(((0, 0), (0, 1), (1, 0), (1, 1))):
            for k in range(H // CROSS_ROWS):
                chunk = i * (H // CROSS_ROWS) + k
                at = (chunk * 4 + plane) * CROSS_ROWS
                top, left = K * r + H * rr + CROSS_ROWS * k, K * c + H * cc
                gram_ref[top : top + CROSS_ROWS, left : left + H] = cross_ref[
                    at : at + CROSS_ROWS, :
                ] * (1.0 / GRID)


def rotation_transposed(gram_ref):
    gram = gram_ref[...]
    y1 = gram[:K] + gram[K:]
    y1t, y1b = y1[:H], y1[H:]
    z1t = dot(y1t, gram)
    m11 = dot_nt(y1t, z1t)

    def metric_rest():
        z1b = dot(y1b, gram)
        yield
        m21 = dot_nt(y1b, z1t)
        yield
        return z1b, m21, dot_nt(y1b, z1b)

    (_, inv1), (z1b, m21, m22) = run_together(cholesky_128(m11), metric_rest())

    y2t = dot(inv1, z1t)

    def first_factor_rest():
        l21 = dot_nt(m21, inv1)
        yield
        _, inv2 = yield from cholesky_128(m22 - dot_nt(l21, l21))
        y2b = dot(inv2, z1b - dot(l21, y2t))
        yield
        return y2b, dot(y2b, gram)

    def second_factors():
        a2t = dot(y2t, gram)
        yield
        p11, e11 = dot_nt(y2t, a2t), dot_nt(a2t, a2t)
        yield
        factors = yield from together(cholesky_128(p11), cholesky_128(e11))
        return a2t, factors

    (y2b, a2b), (a2t, ((_, p_inv1), (e_up1, e_inv1))) = run_together(
        first_factor_rest(), second_factors()
    )
    p_l21 = dot_nt(dot_nt(y2b, a2t), p_inv1)
    e_l21 = dot_nt(dot_nt(a2b, a2t), e_inv1)
    p_rest = dot_nt(y2b, a2b) - dot_nt(p_l21, p_l21)
    e_rest = dot_nt(a2b, a2b) - dot_nt(e_l21, e_l21)

    def frame_top():
        f2t = dot(p_inv1, y2t)
        yield
        solved = y2b - dot(p_l21, f2t)
        yield
        s11 = dot_nt(e_up1, p_inv1)
        yield
        e_u12 = dot(e_inv1, dot_nt(a2t, a2b))
        yield
        s_rest = e_u12 - dot_nt(s11, p_l21)
        yield
        return solved, s_rest, dot(s11, f2t)

    (_, p_inv2), (e_up2, _), (solved, s_rest, rot_top) = run_together(
        cholesky_128(p_rest), cholesky_128(e_rest), frame_top()
    )
    f2b = dot(p_inv2, solved)
    rot_top = rot_top + dot(dot_nt(s_rest, p_inv2), f2b)
    rot_bottom = dot(dot_nt(e_up2, p_inv2), f2b)
    return jnp.concatenate([rot_top, rot_bottom], 0).astype(BF16)


def enter(devices):
    barrier = pltpu.get_barrier_semaphore()
    for device in devices:
        pl.semaphore_signal(barrier, inc=1, device_id=device, device_id_type=MESH)
    pl.semaphore_wait(barrier, len(devices))


def remote(src, dst, sems, index, device):
    copy = pltpu.make_async_remote_copy(
        src_ref=src,
        dst_ref=dst,
        send_sem=sems.at[(0,) + index],
        recv_sem=sems.at[(1,) + index],
        device_id=device,
        device_id_type=MESH,
    )
    copy.start()
    return copy


def span(start, count):
    return pl.ds(pl.multiple_of(start, 8), count)


def store_pieces(part, block, first, per_chunk, offset):
    row = 0
    while row < block.shape[0]:
        chunk, at = divmod(first + row, per_chunk)
        count = min(per_chunk - at, block.shape[0] - row)
        to = chunk * CHUNK + offset + at
        part[to : to + count, :] = block[row : row + count]
        row += count


def merge_kernel(
    own_ref, out_ref, cross_ref, rots_ref, rows_ref, diags_ref, packed_ref, stacked_ref, gram_ref, rot_ref,
    across, part, half, recv0, recv1, sum1, recv2,
    x_sem, core_sem, sem1, sem2, sem_pair, sem_pair_core, sem_x, sem_cross, sem_cross_core,
    sem_own, sem_swap, sem_swap_core,
):
    tm, space = lax.axis_index("tm"), lax.axis_index("space")
    core, y, z = lax.rem(space, 2), lax.rem(lax.div(space, 2), 8), lax.div(space, 16)
    slot = lax.rem(tm, 2)
    sibling = (tm, space + 1 - 2 * core)
    partner = (tm + 1 - 2 * slot, space)
    opposite = (3 - tm, space)

    def on_y(d):
        p = lax.rem(y + d, 8)
        return p, (tm, (z * 8 + p) * 2 + core)

    def on_z(d):
        p = lax.rem(z + d, 8)
        return p, (tm, (p * 8 + y) * 2 + core)

    def on_x(d):
        return lax.rem(tm + d, 4), (lax.rem(tm + d, 4), space)

    first_axis, second_axis = (on_y, on_z), (on_z, on_y)
    first_at, second_at = (y, z), (z, y)
    others = [sibling] + [on_x(d)[1] for d in range(1, 4)]
    for d in range(1, 8):
        others += [on_y(d)[1], on_z(d)[1]]
    load = pltpu.make_async_copy(own_ref, stacked_ref.at[slot], sem_own)
    load.start()
    enter(others)
    load.wait()

    own = stacked_ref.at[slot]
    to_partner = remote(own, own, x_sem, (0,), partner)
    to_opposite = remote(own, across, x_sem, (1,), opposite)
    to_partner.wait()

    tn = ((0,), (0,))
    low, high = stacked_ref[0], stacked_ref[1]
    for base, block in ((0, (low, low)), (3, (high, high)), (6, (low, high))):
        g = bf_dot(block[0], block[1], tn)
        places = ((0, 0), (1, 0), (1, 1)) if base < 6 else ((0, 0), (0, 1), (1, 0), (1, 1))
        for i, (r, c) in enumerate(places):
            block = g[H * r : H * r + H, H * c : H * c + H]
            store_pieces(part, block, H * (base + i), PAIR_ROWS, 0)
    to_opposite.wait()
    first_pair = tm < 2
    left = jnp.where(first_pair, own[...], across[...])
    right = jnp.where(first_pair, across[...], stacked_ref[1 - slot])
    g = bf_dot(left, right, tn)
    for i, (r, c) in enumerate(((0, 0), (0, 1), (1, 0), (1, 1))):
        block = g[H * r : H * r + H, H * c : H * c + H]
        store_pieces(part, block, H * i, CROSS_ROWS, PAIR_ROWS)

    def in_half(h, p):
        return span(h * QUARTER + p * CHUNK, CHUNK)

    order = [(h, d) for d in FAR_FIRST + (0,) for h in range(2)]
    halves, copies = [], []
    for h, d in order:
        p = lax.rem(first_at[h] + d, 8)
        theirs = part.at[span((1 - core) * HALF + h * QUARTER + p * CHUNK, CHUNK)]
        halves.append(remote(theirs, recv0.at[in_half(h, p)], core_sem, (h, d), sibling))
    for (h, d), copy in zip(order, halves):
        copy.wait()
        p = lax.rem(first_at[h] + d, 8)
        mine = span(core * HALF + h * QUARTER + p * CHUNK, CHUNK)
        total = part[mine, :] + recv0[in_half(h, p), :]
        if d:
            half[in_half(h, p), :] = total
            to = first_axis[h](d)[1]
            copies.append(remote(half.at[in_half(h, p)], recv1.at[h, first_at[h]], sem1, (h, d), to))
        else:
            recv1[h, p] = total
    for copy in copies:
        copy.wait()
    for h in range(2):
        total = recv1[h, 0]
        for p in range(1, 8):
            total = total + recv1[h, p]
        sum1[h] = total

    copies = []
    for d in FAR_FIRST:
        for h in range(2):
            device = second_axis[h](d)[1]
            copies.append(remote(sum1.at[h], recv2.at[h, second_at[h]], sem2, (h, d), device))
    for h in range(2):
        recv2[h, second_at[h]] = sum1[h]
    for copy in copies:
        copy.wait()

    def chunk(h, p):
        return core * (CHUNKS // 2) + h * (CHUNKS // 4) + p

    def pair_at(h, p):
        return packed_ref.at[span(chunk(h, p) * PAIR_ROWS, PAIR_ROWS)]

    def cross_at(h, p):
        return cross_ref.at[span(chunk(h, p) * 4 * CROSS_ROWS, 4 * CROSS_ROWS)]

    def plane_at(h, plane):
        start = (chunk(h, first_at[h]) * 4 + plane) * CROSS_ROWS
        return cross_ref.at[span(start, CROSS_ROWS)]

    for h in range(2):
        total = recv2[h, 0]
        for p in range(1, 8):
            total = total + recv2[h, p]
        pair_at(h, first_at[h])[...] = total[:PAIR_ROWS]
        plane_at(h, tm)[...] = total[PAIR_ROWS:]

    along_x, pairs, crosses, forwards = [], [], [], []
    for d in range(1, 4):
        for h in range(2):
            mine = plane_at(h, tm)
            along_x.append(remote(mine, mine, sem_x, (h, d), on_x(d)[1]))
    for d in FAR_FIRST:
        for h in range(2):
            mine = pair_at(h, first_at[h])
            pairs.append((h, d, remote(mine, mine, sem_pair, (h, d), first_axis[h](d)[1])))
    for h in range(2):
        mine = pair_at(h, first_at[h])
        forwards.append(remote(mine, mine, sem_pair_core, (h, 0), sibling))
    for copy in along_x:
        copy.wait()
    for d in FAR_FIRST:
        for h in range(2):
            mine = cross_at(h, first_at[h])
            crosses.append((h, d, remote(mine, mine, sem_cross, (h, d), first_axis[h](d)[1])))

    def forward(copies, at, sems):
        for h, d, copy in copies[::-1]:
            copy.wait()
            arrived = at(h, lax.rem(first_at[h] + 8 - d, 8))
            forwards.append(remote(arrived, arrived, sems, (h, d), sibling))

    forward(pairs, pair_at, sem_pair_core)
    for copy in forwards:
        copy.wait()

    unpack_pair(packed_ref, gram_ref)
    rot = rotation_transposed(gram_ref)
    side = lax.div(tm, 2)
    rots_ref[side] = rot
    diag_rows = 3 * H // 2
    diag_part = span(core * diag_rows, diag_rows)

    def rot_at(side, i):
        count = K // 2 // SWAP_PIECES
        start = core * (K // 2) + i * count
        return rots_ref.at[side, pl.ds(pl.multiple_of(start, 16), count)]

    swap_rots = []
    for i in range(SWAP_PIECES):
        mine = rot_at(side, i)
        swap_rots.append(remote(mine, mine, sem_swap, (i,), opposite))
    diag = rounded_right_nt(rounded_left(rot, gram_ref[...]), rot)
    for i, (r, c) in enumerate(((0, 0), (1, 0), (1, 1))):
        diags_ref[side, H * i : H * i + H, :] = diag[H * r : H * r + H, H * c : H * c + H]
    mine = diags_ref.at[side, diag_part]
    swap_diags = remote(mine, mine, sem_swap, (SWAP_PIECES,), opposite)
    forwards = []
    for h in range(2):
        mine = cross_at(h, first_at[h])
        forwards.append(remote(mine, mine, sem_cross_core, (h, 0), sibling))
    forward(crosses, cross_at, sem_cross_core)
    nt = ((1,), (1,))
    rows_ref[side] = (
        bf_dot(stacked_ref[0], rot[:, :K], nt) + bf_dot(stacked_ref[1], rot[:, K:], nt)
    ).astype(BF16)
    mine = rows_ref.at[side]
    swap_rows = remote(mine, mine, sem_swap, (SWAP_PIECES + 1,), opposite)
    shares = []
    for i, copy in enumerate(swap_rots):
        copy.wait()
        arrived = rot_at(1 - side, i)
        shares.append(remote(arrived, arrived, sem_swap_core, (i,), sibling))
    for copy in forwards:
        copy.wait()
    unpack_cross(cross_ref, gram_ref)
    swap_diags.wait()
    arrived = diags_ref.at[1 - side, diag_part]
    shares.append(remote(arrived, arrived, sem_swap_core, (SWAP_PIECES,), sibling))
    for copy in shares:
        copy.wait()

    cross = rounded_right_nt(rounded_left(rots_ref[0], gram_ref[...]), rots_ref[1])
    gram_ref[:K, K:] = cross
    gram_ref[K:, :K] = cross.T
    for i in range(2):
        b = [diags_ref[i, H * k : H * k + H, :] for k in range(3)]
        put(gram_ref, 2 * i, 2 * i, b[0])
        put(gram_ref, 2 * i + 1, 2 * i, b[1])
        put(gram_ref, 2 * i, 2 * i + 1, b[1].T)
        put(gram_ref, 2 * i + 1, 2 * i + 1, b[2])
    rot_ref[...] = rotation_transposed(gram_ref)
    width = out_ref.shape[0]
    rot = rot_ref[pl.ds(pl.multiple_of(tm * width, width), width), :]
    swap_rows.wait()
    out_ref[...] = bf_dot(rot[:, :K], rows_ref[0], nt) + bf_dot(rot[:, K:], rows_ref[1], nt)


def merge(own):
    dma = pltpu.SemaphoreType.DMA
    return pl.pallas_call(
        merge_kernel,
        out_shape=jax.ShapeDtypeStruct((K // 4, 256), F32),
        in_specs=[pl.BlockSpec(memory_space=pltpu.HBM)],
        out_specs=pl.BlockSpec(memory_space=pltpu.VMEM),
        scratch_shapes=[
            pltpu.VMEM((4 * CROSS, H), F32),
            pltpu.VMEM((2, K, 2 * K), BF16),
            pltpu.VMEM((2, 256, K), BF16),
            pltpu.VMEM((2, 3 * H, H), F32),
            pltpu.VMEM((PAIR, H), F32),
            pltpu.VMEM((2, 256, K), BF16),
            pltpu.VMEM((2 * K, 2 * K), F32),
            pltpu.VMEM((K, 2 * K), BF16),
            pltpu.VMEM((256, K), BF16),
            pltpu.VMEM((ROWS, H), F32),
            pltpu.VMEM((HALF, H), F32),
            pltpu.VMEM((HALF, H), F32),
            pltpu.VMEM((2, 8, CHUNK, H), F32),
            pltpu.VMEM((2, CHUNK, H), F32),
            pltpu.VMEM((2, 8, CHUNK, H), F32),
            dma((2, 2)),
            dma((2, 2, 8)),
            dma((2, 2, 8)),
            dma((2, 2, 8)),
            dma((2, 2, 8)),
            dma((2, 2, 8)),
            dma((2, 2, 4)),
            dma((2, 2, 8)),
            dma((2, 2, 8)),
            dma(()),
            dma((2, SWAP_PIECES + 2)),
            dma((2, SWAP_PIECES + 1)),
        ],
        compiler_params=pltpu.CompilerParams(
            collective_id=0, has_side_effects=True, vmem_limit_bytes=VMEM_LIMIT
        ),
        name="merge_all",
    )(own)


def body(bases):
    return merge(bases[0]).T


def solution(mesh):
    return jax.shard_map(
        body,
        mesh=mesh,
        in_specs=(P("tm", "space", None),),
        out_specs=P("space", "tm"),
        check_vma=False,
    )
```

```python
import functools

import jax
import jax.numpy as jnp
from jax import lax
from jax.experimental import pallas as pl
from jax.experimental.pallas import tpu as pltpu
from jax.sharding import PartitionSpec as P

MESH = pl.DeviceIdType.MESH
F32 = jnp.float32
BF16 = jnp.bfloat16
K = 256
H = 128
GRID = 32768
PAIR_ROWS = 40
CROSS_ROWS = 16
CHUNK = PAIR_ROWS + CROSS_ROWS
CHUNKS = 32
PAIR = PAIR_ROWS * CHUNKS
CROSS = CROSS_ROWS * CHUNKS
ROWS = CHUNK * CHUNKS
QUARTER = ROWS // 4
HALF = ROWS // 2
SWAP_PIECES = 4
FAR_FIRST = (4, 3, 5, 2, 6, 1, 7)
VMEM_LIMIT = 60 * 1024 * 1024


def dot(a, b, dims=((1,), (0,))):
    return lax.dot_general(
        a,
        b,
        (dims, ((), ())),
        precision=lax.Precision.HIGHEST,
        preferred_element_type=F32,
    )


def dot_nt(a, b):
    return dot(a, b, ((1,), (1,)))


def dot_tn(a, b):
    return dot(a, b, ((0,), (0,)))


def lane_bc(x, c):
    return jnp.broadcast_to(x[:, c : c + 1], x.shape)


def sub_bc(x, r):
    return jnp.broadcast_to(x[r : r + 1, :], x.shape)


def weighted(cols, rows):
    s0 = cols[0] * rows[0]
    s1 = cols[1] * rows[1]
    for c in range(2, 8, 2):
        s0 = s0 + cols[c] * rows[c]
        s1 = s1 + cols[c + 1] * rows[c + 1]
    return s0 + s1


def factor_block(w, offset):
    groups = 8
    sub = lax.broadcasted_iota(jnp.int32, (8, 128), 0)
    rows = [w[8 * g : 8 * g + 8] for g in range(groups)]
    done = []
    pending = []

    def spread(h, g):
        return [lane_bc(rows[h], offset + 8 * g + c) for c in range(8)]

    def update(h, cols, v):
        rows[h] = rows[h] - weighted(cols, v)

    p = spread(0, 0)
    below, ahead = spread(1, 0), spread(1, 1)
    later = {h: spread(h, 0) for h in range(2, groups)}
    for g in range(groups):
        jordan = forward = rows[g]
        recips = jnp.ones_like(jordan)
        last = g == groups - 1
        raw = list(below)
        for j in range(8):
            r = 1.0 / sub_bc(p[j], j)
            f = p[j] * r
            f_all = jnp.where(sub != j, f, 0.0)
            if not last:
                f_next = below[j] * r
                row_next = [sub_bc(below[j], c) for c in range(8)]
            for c in range(j + 1, 8):
                row = sub_bc(p[c], j)
                p[c] = p[c] - f_all * row
                if not last:
                    below[c] = below[c] - f_next * row
            if not last:
                ahead = [a - f_next * x for a, x in zip(ahead, row_next)]
            x = sub_bc(jordan, j)
            jordan = jordan - f_all * x
            if j < 7:
                forward = forward - jnp.where(sub > j, f, 0.0) * x
            recips = jnp.where(sub == j, r, recips)
            if pending:
                pending.pop(0)()
            yield None
        while pending:
            pending.pop(0)()
        done.append(forward * jnp.sqrt(recips))
        if last:
            break
        v = jordan * recips
        v = [sub_bc(v, c) for c in range(8)]
        p = ahead
        if g + 2 < groups:
            update(g + 2, later.pop(g + 2), v)
            below, ahead = spread(g + 2, g + 1), spread(g + 2, g + 2)
        update(g + 1, raw, v)

        def finish(h, g=g, v=v):
            update(h, later.pop(h), v)
            later[h] = spread(h, g + 1)

        pending = [functools.partial(finish, h) for h in range(g + 3, groups)]
    return jnp.concatenate(done, 0)


def cholesky_128(a):
    half = H // 2
    row = lax.broadcasted_iota(jnp.int32, (half, H), 0)
    lane = lax.broadcasted_iota(jnp.int32, (half, H), 1)
    low = lane < half
    one, zero = jnp.ones((half, H), F32), jnp.zeros((half, H), F32)
    top, bottom = a[:half], a[half:]
    w = jnp.where(low, top, jnp.where(lane == row + half, one, zero))
    f1 = yield from factor_block(w, 0)
    inv1 = pltpu.roll(jnp.where(low, 0.0, f1), half, 1)
    l21 = dot_nt(bottom, inv1)
    yield
    rest = bottom - dot_nt(l21, jnp.concatenate([jnp.zeros((half, half), F32), l21], 0))
    w = jnp.where(low, jnp.where(lane == row, one, zero), rest)
    yield
    q = dot(l21, inv1)
    u1 = dot(inv1[:, :half], top)
    f2 = yield from factor_block(w, half)
    inv2 = jnp.where(low, f2, 0.0)
    x = dot(inv2[:, :half], q)
    inverse = jnp.concatenate([inv1, pltpu.roll(inv2, half, 1) - x], 0)
    upper = jnp.concatenate(
        [jnp.where(lane >= row, u1, 0.0), jnp.where(lane >= row + half, f2, 0.0)], 0
    )
    return upper, inverse


def together(*steps):
    results = [None] * len(steps)
    running = list(enumerate(steps))
    while running:
        for item in list(running):
            try:
                next(item[1])
            except StopIteration as end:
                results[item[0]] = end.value
                running.remove(item)
        yield
    return results


def run_together(*steps):
    work = together(*steps)
    while True:
        try:
            next(work)
        except StopIteration as end:
            return end.value


def split3(x):
    hi = x.astype(BF16)
    rest = x - hi.astype(F32)
    mid = rest.astype(BF16)
    low = (rest - mid.astype(F32)).astype(BF16)
    return hi, mid, low


def bf_dot(a, b, dims=((1,), (0,))):
    return lax.dot_general(a, b, (dims, ((), ())), preferred_element_type=F32)


def rounded_left(a, x):
    hi, mid, low = split3(x)
    return bf_dot(a, low) + bf_dot(a, mid) + bf_dot(a, hi)


def rounded_right_nt(x, a):
    nt = ((1,), (1,))
    hi, mid, low = split3(x)
    return bf_dot(low, a, nt) + bf_dot(mid, a, nt) + bf_dot(hi, a, nt)


def put(ref, r, c, block):
    ref[H * r : H * r + H, H * c : H * c + H] = block


def unpack_pair(packed_ref, gram_ref):
    b = [packed_ref[H * i : H * i + H, :] * (1.0 / GRID) for i in range(10)]
    for base, at in ((0, 0), (3, 2)):
        put(gram_ref, at, at, b[base])
        put(gram_ref, at + 1, at, b[base + 1])
        put(gram_ref, at, at + 1, b[base + 1].T)
        put(gram_ref, at + 1, at + 1, b[base + 2])
    for i, (r, c) in enumerate(((0, 2), (0, 3), (1, 2), (1, 3))):
        put(gram_ref, r, c, b[6 + i])
        put(gram_ref, c, r, b[6 + i].T)


CROSS_AT = ((0, 1), (1, 0), (1, 1), (0, 0))


def unpack_cross(cross_ref, gram_ref):
    for plane, (r, c) in enumerate(CROSS_AT):
        for i, (rr, cc) in enumerate(((0, 0), (0, 1), (1, 0), (1, 1))):
            for k in range(H // CROSS_ROWS):
                chunk = i * (H // CROSS_ROWS) + k
                at = (chunk * 4 + plane) * CROSS_ROWS
                top, left = K * r + H * rr + CROSS_ROWS * k, K * c + H * cc
                gram_ref[top : top + CROSS_ROWS, left : left + H] = cross_ref[
                    at : at + CROSS_ROWS, :
                ] * (1.0 / GRID)


def rotation_transposed(gram_ref):
    gram = gram_ref[...]
    y1 = gram[:K] + gram[K:]
    y1t, y1b = y1[:H], y1[H:]
    z1t = dot(y1t, gram)
    m11 = dot_nt(y1t, z1t)

    def metric_rest():
        z1b = dot(y1b, gram)
        yield
        m21 = dot_nt(y1b, z1t)
        yield
        return z1b, m21, dot_nt(y1b, z1b)

    (_, inv1), (z1b, m21, m22) = run_together(cholesky_128(m11), metric_rest())

    y2t = dot(inv1, z1t)

    def first_factor_rest():
        l21 = dot_nt(m21, inv1)
        yield
        _, inv2 = yield from cholesky_128(m22 - dot_nt(l21, l21))
        y2b = dot(inv2, z1b - dot(l21, y2t))
        yield
        return y2b, dot(y2b, gram)

    def second_factors():
        a2t = dot(y2t, gram)
        yield
        p11, e11 = dot_nt(y2t, a2t), dot_nt(a2t, a2t)
        yield
        factors = yield from together(cholesky_128(p11), cholesky_128(e11))
        return a2t, factors

    (y2b, a2b), (a2t, ((_, p_inv1), (e_up1, e_inv1))) = run_together(
        first_factor_rest(), second_factors()
    )
    p_l21 = dot_nt(dot_nt(y2b, a2t), p_inv1)
    e_l21 = dot_nt(dot_nt(a2b, a2t), e_inv1)
    p_rest = dot_nt(y2b, a2b) - dot_nt(p_l21, p_l21)
    e_rest = dot_nt(a2b, a2b) - dot_nt(e_l21, e_l21)

    def frame_top():
        f2t = dot(p_inv1, y2t)
        yield
        solved = y2b - dot(p_l21, f2t)
        yield
        s11 = dot_nt(e_up1, p_inv1)
        yield
        e_u12 = dot(e_inv1, dot_nt(a2t, a2b))
        yield
        s_rest = e_u12 - dot_nt(s11, p_l21)
        yield
        return solved, s_rest, dot(s11, f2t)

    (_, p_inv2), (e_up2, _), (solved, s_rest, rot_top) = run_together(
        cholesky_128(p_rest), cholesky_128(e_rest), frame_top()
    )
    f2b = dot(p_inv2, solved)
    rot_top = rot_top + dot(dot_nt(s_rest, p_inv2), f2b)
    rot_bottom = dot(dot_nt(e_up2, p_inv2), f2b)
    return jnp.concatenate([rot_top, rot_bottom], 0).astype(BF16)


def enter(devices):
    barrier = pltpu.get_barrier_semaphore()
    for device in devices:
        pl.semaphore_signal(barrier, inc=1, device_id=device, device_id_type=MESH)
    pl.semaphore_wait(barrier, len(devices))


def remote(src, dst, sems, index, device):
    copy = pltpu.make_async_remote_copy(
        src_ref=src,
        dst_ref=dst,
        send_sem=sems.at[(0,) + index],
        recv_sem=sems.at[(1,) + index],
        device_id=device,
        device_id_type=MESH,
    )
    copy.start()
    return copy


def span(start, count):
    return pl.ds(pl.multiple_of(start, 8), count)


def store_pieces(part, block, first, per_chunk, offset):
    row = 0
    while row < block.shape[0]:
        chunk, at = divmod(first + row, per_chunk)
        count = min(per_chunk - at, block.shape[0] - row)
        to = chunk * CHUNK + offset + at
        part[to : to + count, :] = block[row : row + count]
        row += count


def merge_kernel(
    own_ref, out_ref, cross_ref, rots_ref, rows_ref, diags_ref, packed_ref, stacked_ref, gram_ref, rot_ref,
    across, part, half, recv0, recv1, sum1, recv2,
    x_sem, core_sem, sem1, sem1_cross, sem2, sem2_cross, sem_pair, sem_pair_core, sem_x, sem_cross, sem_cross_core,
    sem_own, sem_swap, sem_swap_core,
):
    tm, space = lax.axis_index("tm"), lax.axis_index("space")
    core, y, z = lax.rem(space, 2), lax.rem(lax.div(space, 2), 8), lax.div(space, 16)
    slot = lax.rem(tm, 2)
    sibling = (tm, space + 1 - 2 * core)
    partner = (tm + 1 - 2 * slot, space)
    opposite = (3 - tm, space)

    def on_y(d):
        p = lax.rem(y + d, 8)
        return p, (tm, (z * 8 + p) * 2 + core)

    def on_z(d):
        p = lax.rem(z + d, 8)
        return p, (tm, (p * 8 + y) * 2 + core)

    def on_x(d):
        return lax.rem(tm + d, 4), (lax.rem(tm + d, 4), space)

    first_axis, second_axis = (on_y, on_z), (on_z, on_y)
    first_at, second_at = (y, z), (z, y)
    others = [sibling] + [on_x(d)[1] for d in range(1, 4)]
    for d in range(1, 8):
        others += [on_y(d)[1], on_z(d)[1]]
    load = pltpu.make_async_copy(own_ref, stacked_ref.at[slot], sem_own)
    load.start()
    enter(others)
    load.wait()

    own = stacked_ref.at[slot]
    to_partner = remote(own, own, x_sem, (0,), partner)
    to_opposite = remote(own, across, x_sem, (1,), opposite)
    to_partner.wait()

    tn = ((0,), (0,))
    low, high = stacked_ref[0], stacked_ref[1]
    for base, block in ((0, (low, low)), (3, (high, high)), (6, (low, high))):
        g = bf_dot(block[0], block[1], tn)
        places = ((0, 0), (1, 0), (1, 1)) if base < 6 else ((0, 0), (0, 1), (1, 0), (1, 1))
        for i, (r, c) in enumerate(places):
            block = g[H * r : H * r + H, H * c : H * c + H]
            store_pieces(part, block, H * (base + i), PAIR_ROWS, 0)
    to_opposite.wait()
    first_pair = tm < 2
    left = jnp.where(first_pair, own[...], across[...])
    right = jnp.where(first_pair, across[...], stacked_ref[1 - slot])
    g = bf_dot(left, right, tn)
    for i, (r, c) in enumerate(((0, 0), (0, 1), (1, 0), (1, 1))):
        block = g[H * r : H * r + H, H * c : H * c + H]
        store_pieces(part, block, H * i, CROSS_ROWS, PAIR_ROWS)

    def in_half(h, p):
        return span(h * QUARTER + p * CHUNK, CHUNK)

    order = [(h, d) for d in FAR_FIRST + (0,) for h in range(2)]
    to_pair, to_cross = pl.ds(0, PAIR_ROWS), pl.ds(PAIR_ROWS, CROSS_ROWS)
    halves, copies, late = [], [], []
    for h, d in order:
        p = lax.rem(first_at[h] + d, 8)
        theirs = part.at[span((1 - core) * HALF + h * QUARTER + p * CHUNK, CHUNK)]
        halves.append(remote(theirs, recv0.at[in_half(h, p)], core_sem, (h, d), sibling))
    for (h, d), copy in zip(order, halves):
        copy.wait()
        p = lax.rem(first_at[h] + d, 8)
        mine = span(core * HALF + h * QUARTER + p * CHUNK, CHUNK)
        total = part[mine, :] + recv0[in_half(h, p), :]
        if d:
            half[in_half(h, p), :] = total
            source = half.at[span(h * QUARTER + p * CHUNK, PAIR_ROWS)]
            target = recv1.at[h, first_at[h], to_pair]
            copies.append(remote(source, target, sem1, (h, d), first_axis[h](d)[1]))
        else:
            recv1[h, p] = total
    for h, d in order[:-2]:
        p, to = first_axis[h](d)
        source = half.at[span(h * QUARTER + p * CHUNK + PAIR_ROWS, CROSS_ROWS)]
        target = recv1.at[h, first_at[h], to_cross]
        late.append(remote(source, target, sem1_cross, (h, d), to))

    def sum_first(copies, first, count):
        for copy in copies:
            copy.wait()
        for h in range(2):
            total = recv1[h, 0, first : first + count, :]
            for p in range(1, 8):
                total = total + recv1[h, p, first : first + count, :]
            sum1[h, first : first + count, :] = total
            recv2[h, second_at[h], first : first + count, :] = total

    def send_second(at, sems):
        sent = []
        for h, d in order[:-2]:
            target = recv2.at[h, second_at[h], at]
            sent.append(remote(sum1.at[h, at], target, sems, (h, d), second_axis[h](d)[1]))
        return sent

    def sum_second(h, first, count):
        total = recv2[h, 0, first : first + count, :]
        for p in range(1, 8):
            total = total + recv2[h, p, first : first + count, :]
        return total

    sum_first(copies, 0, PAIR_ROWS)
    copies = send_second(to_pair, sem2)
    sum_first(late, PAIR_ROWS, CROSS_ROWS)
    late = send_second(to_cross, sem2_cross)

    def chunk(h, p):
        return core * (CHUNKS // 2) + h * (CHUNKS // 4) + p

    def pair_at(h, p):
        return packed_ref.at[span(chunk(h, p) * PAIR_ROWS, PAIR_ROWS)]

    def cross_at(h, p):
        return cross_ref.at[span(chunk(h, p) * 4 * CROSS_ROWS, 4 * CROSS_ROWS)]

    def plane_at(h, plane):
        start = (chunk(h, first_at[h]) * 4 + plane) * CROSS_ROWS
        return cross_ref.at[span(start, CROSS_ROWS)]

    along_x, pairs, crosses, forwards = [], [], [], []
    for copy in copies:
        copy.wait()
    for h in range(2):
        pair_at(h, first_at[h])[...] = sum_second(h, 0, PAIR_ROWS)
    for h, d in order[:-2]:
        mine = pair_at(h, first_at[h])
        pairs.append((h, d, remote(mine, mine, sem_pair, (h, d), first_axis[h](d)[1])))
    for h in range(2):
        mine = pair_at(h, first_at[h])
        forwards.append(remote(mine, mine, sem_pair_core, (h, 0), sibling))
    for copy in late:
        copy.wait()
    for h in range(2):
        plane_at(h, tm)[...] = sum_second(h, PAIR_ROWS, CROSS_ROWS)
    for d in range(1, 4):
        for h in range(2):
            mine = plane_at(h, tm)
            along_x.append(remote(mine, mine, sem_x, (h, d), on_x(d)[1]))
    for copy in along_x:
        copy.wait()
    for d in FAR_FIRST:
        for h in range(2):
            mine = cross_at(h, first_at[h])
            crosses.append((h, d, remote(mine, mine, sem_cross, (h, d), first_axis[h](d)[1])))

    def forward(copies, at, sems):
        for h, d, copy in copies[::-1]:
            copy.wait()
            arrived = at(h, lax.rem(first_at[h] + 8 - d, 8))
            forwards.append(remote(arrived, arrived, sems, (h, d), sibling))

    forward(pairs, pair_at, sem_pair_core)
    for copy in forwards:
        copy.wait()

    unpack_pair(packed_ref, gram_ref)
    rot = rotation_transposed(gram_ref)
    side = lax.div(tm, 2)
    rots_ref[side] = rot
    diag_rows = 3 * H // 2
    diag_part = span(core * diag_rows, diag_rows)

    def rot_at(side, i):
        count = K // 2 // SWAP_PIECES
        start = core * (K // 2) + i * count
        return rots_ref.at[side, pl.ds(pl.multiple_of(start, 16), count)]

    swap_rots = []
    for i in range(SWAP_PIECES):
        mine = rot_at(side, i)
        swap_rots.append(remote(mine, mine, sem_swap, (i,), opposite))
    diag = rounded_right_nt(rounded_left(rot, gram_ref[...]), rot)
    for i, (r, c) in enumerate(((0, 0), (1, 0), (1, 1))):
        diags_ref[side, H * i : H * i + H, :] = diag[H * r : H * r + H, H * c : H * c + H]
    mine = diags_ref.at[side, diag_part]
    swap_diags = remote(mine, mine, sem_swap, (SWAP_PIECES,), opposite)
    forwards = []
    for h in range(2):
        mine = cross_at(h, first_at[h])
        forwards.append(remote(mine, mine, sem_cross_core, (h, 0), sibling))
    forward(crosses, cross_at, sem_cross_core)
    nt = ((1,), (1,))
    rows_ref[side] = (
        bf_dot(stacked_ref[0], rot[:, :K], nt) + bf_dot(stacked_ref[1], rot[:, K:], nt)
    ).astype(BF16)
    mine = rows_ref.at[side]
    swap_rows = remote(mine, mine, sem_swap, (SWAP_PIECES + 1,), opposite)
    shares = []
    for i, copy in enumerate(swap_rots):
        copy.wait()
        arrived = rot_at(1 - side, i)
        shares.append(remote(arrived, arrived, sem_swap_core, (i,), sibling))
    for copy in forwards:
        copy.wait()
    unpack_cross(cross_ref, gram_ref)
    swap_diags.wait()
    arrived = diags_ref.at[1 - side, diag_part]
    shares.append(remote(arrived, arrived, sem_swap_core, (SWAP_PIECES,), sibling))
    for copy in shares:
        copy.wait()

    cross = rounded_right_nt(rounded_left(rots_ref[0], gram_ref[...]), rots_ref[1])
    gram_ref[:K, K:] = cross
    gram_ref[K:, :K] = cross.T
    for i in range(2):
        b = [diags_ref[i, H * k : H * k + H, :] for k in range(3)]
        put(gram_ref, 2 * i, 2 * i, b[0])
        put(gram_ref, 2 * i + 1, 2 * i, b[1])
        put(gram_ref, 2 * i, 2 * i + 1, b[1].T)
        put(gram_ref, 2 * i + 1, 2 * i + 1, b[2])
    rot_ref[...] = rotation_transposed(gram_ref)
    width = out_ref.shape[0]
    rot = rot_ref[pl.ds(pl.multiple_of(tm * width, width), width), :]
    swap_rows.wait()
    out_ref[...] = bf_dot(rot[:, :K], rows_ref[0], nt) + bf_dot(rot[:, K:], rows_ref[1], nt)


def merge(own):
    dma = pltpu.SemaphoreType.DMA
    return pl.pallas_call(
        merge_kernel,
        out_shape=jax.ShapeDtypeStruct((K // 4, 256), F32),
        in_specs=[pl.BlockSpec(memory_space=pltpu.HBM)],
        out_specs=pl.BlockSpec(memory_space=pltpu.VMEM),
        scratch_shapes=[
            pltpu.VMEM((4 * CROSS, H), F32),
            pltpu.VMEM((2, K, 2 * K), BF16),
            pltpu.VMEM((2, 256, K), BF16),
            pltpu.VMEM((2, 3 * H, H), F32),
            pltpu.VMEM((PAIR, H), F32),
            pltpu.VMEM((2, 256, K), BF16),
            pltpu.VMEM((2 * K, 2 * K), F32),
            pltpu.VMEM((K, 2 * K), BF16),
            pltpu.VMEM((256, K), BF16),
            pltpu.VMEM((ROWS, H), F32),
            pltpu.VMEM((HALF, H), F32),
            pltpu.VMEM((HALF, H), F32),
            pltpu.VMEM((2, 8, CHUNK, H), F32),
            pltpu.VMEM((2, CHUNK, H), F32),
            pltpu.VMEM((2, 8, CHUNK, H), F32),
            dma((2, 2)),
            dma((2, 2, 8)),
            dma((2, 2, 8)),
            dma((2, 2, 8)),
            dma((2, 2, 8)),
            dma((2, 2, 8)),
            dma((2, 2, 8)),
            dma((2, 2, 8)),
            dma((2, 2, 4)),
            dma((2, 2, 8)),
            dma((2, 2, 8)),
            dma(()),
            dma((2, SWAP_PIECES + 2)),
            dma((2, SWAP_PIECES + 1)),
        ],
        compiler_params=pltpu.CompilerParams(
            collective_id=0, has_side_effects=True, vmem_limit_bytes=VMEM_LIMIT
        ),
        name="merge_all",
    )(own)


def body(bases):
    return merge(bases[0]).T


def solution(mesh):
    return jax.shard_map(
        body,
        mesh=mesh,
        in_specs=(P("tm", "space", None),),
        out_specs=P("space", "tm"),
        check_vma=False,
    )
```
